256 devices in a mesh: grp: 4 (over x), blk: 64 (over z, y, core).
Axes of the slice: x: 4, y: 4, z: 8, core: 2. Of those that a mesh axis runs over, the one named last changes fastest.
Arguments:
- embeddings: bfloat16 [32768, 1024], P(('grp', 'blk')), may hold values from -6 to 6
- cluster_ids: int32 [32768], P(('grp', 'blk')), may hold values from 0 to 15, as said below
- row_order: int32 [32768], P(('grp', 'blk')), may hold values from 0 to 32767, each once
Outputs:
- nearest_earlier: float32 [32768], P(('grp', 'blk'))
The draws below stay inside these ranges and needn't reach their ends.
Inputs may be any that keep to these rules, and one draw needn't show every extreme that they name: `cluster_ids`: in each aligned block of 128 rows (the rows of one device), at most 64 rows have ids with one value of id % 4, and at most 16 rows have one id. For every blk index some value of id % 4 is taken by exactly 64 rows of every block placed on a device with that blk index, each of its 4 ids by exactly 16 of them.
All inputs are finite; a program needn't handle non-finite values.
Results may differ from the reference program's by a relative error of at most 0.0014.
Values may be sent and summed in bfloat16 or wider, within the bound.
A program may use at most 128 MiB of HBM per device.

```python
import jax
import jax.numpy as jnp
from jax import lax

D = 1024
ROWS_DEV = 128
CPG = 4
ROWS = 32768
N_GRP = 4
N_BLK = 64


def draw_cluster_ids(key, part):
    key = jax.random.fold_in(key, 11)
    first, second, third, fourth = jax.random.split(key, 4)
    devices = N_GRP * N_BLK
    capacity = 2 * ROWS_DEV // N_GRP
    slots = N_GRP * capacity
    lane = jnp.arange(devices) % N_BLK
    favored = jax.random.randint(first, (N_BLK,), 0, N_GRP)[lane]
    owner = jnp.arange(slots) // capacity
    score = jax.random.randint(second, (devices, slots), 0, 2 ** 16) * slots + jnp.arange(slots)[None, :]
    score = jnp.where(owner[None, :] == favored[:, None], score - 2 ** 30, score)
    picked = jnp.argsort(score, axis=1, stable=True)[:, :ROWS_DEV]
    mixing = jax.random.randint(third, (devices, ROWS_DEV), 0, 2 ** 16) * ROWS_DEV + jnp.arange(ROWS_DEV)[None, :]
    shuffle = jnp.argsort(mixing, axis=1, stable=True)
    picked = jnp.take_along_axis(picked, shuffle, axis=1)
    target = picked // capacity
    onehot = (target[:, :, None] == jnp.arange(N_GRP)[None, None, :]).astype(jnp.int32)
    ranked = jnp.sum(onehot * (jnp.cumsum(onehot, axis=1) - 1), axis=2)
    offset = jax.random.randint(fourth, (devices, 1), 0, CPG)
    member = (ranked + offset) % CPG
    return (target + N_GRP * member).reshape(-1).astype(jnp.int32)


def block_scale(stream_key, dims, cuts, smallest, top_value):
    factor_of = 1.0
    for position, shards_of in cuts:
        draws = jax.random.uniform(jax.random.fold_in(jax.random.fold_in(stream_key, 6), position), (shards_of,), jnp.float32, smallest / len(cuts), top_value / len(cuts))
        factor_of = factor_of * jnp.repeat(jnp.exp(draws), dims[position] // shards_of).reshape((-1,) + (1,) * (len(dims) - 1 - position))
    return factor_of


def noise(rng, extent, scale, bound, shards=(), held_as=jnp.bfloat16):
    drawn = scale * jax.random.normal(rng, extent, jnp.float32)
    if shards:
        drawn = drawn * block_scale(rng, extent, shards, -0.22, 0.18)
    return jnp.clip(drawn, -bound, bound).astype(held_as)


def setup_inputs(seed: int = 0) -> dict:
    keys = jax.random.split(jax.random.key(seed), 4)
    embeddings = noise(keys[0], (ROWS, D), 1.0, 6.0, ((0, 256),))
    cluster_ids = draw_cluster_ids(jax.random.fold_in(keys[3], 71), 0)
    row_order = jax.random.permutation(keys[2], ROWS).astype(jnp.int32)
    return {"embeddings": embeddings, "cluster_ids": cluster_ids, "row_order": row_order}


def reference(embeddings, cluster_ids, row_order):
    values = embeddings.astype(jnp.float32)
    unit = (values * lax.rsqrt(lax.optimization_barrier(jnp.sum(values * values, axis=1, keepdims=True)) + 1e-06)).astype(jnp.bfloat16)
    unit = lax.optimization_barrier(unit).astype(jnp.float32)
    width = unit.shape[1]
    block = min(512, ROWS)

    def one_block(pieces):
        rows_unit, rows_cluster, rows_order = pieces
        similarity = jnp.dot(rows_unit, unit.T, precision=lax.Precision.HIGHEST, preferred_element_type=jnp.float32)
        mask = (rows_cluster[:, None] == cluster_ids[None, :]) & (row_order[None, :] < rows_order[:, None])
        return lax.optimization_barrier(jnp.max(jnp.where(mask, similarity, jnp.float32(-1.0)), axis=1))
    result = lax.map(one_block, (unit.reshape(ROWS // block, block, width), cluster_ids.reshape(ROWS // block, block), row_order.reshape(ROWS // block, block)))
    return result.reshape(ROWS)
```

```python
import functools
import jax
import jax.numpy as jnp
from jax import lax
from jax.experimental import pallas as pl
from jax.experimental.pallas import tpu as pltpu
from jax.sharding import PartitionSpec as P

MESH = pl.DeviceIdType.MESH
NX, NY, NZ = 4, 4, 8
CHUNKS = 65
HALF = ((0, 32), (32, 33))
OFF = (0, -1, 1, 2)
ZOFF = (0, -1, 1, -2, 2, -3, 3, 4)


def slot_c(a, b):
    return OFF.index(a) * 4 + OFF.index(b)


def wide(ref, start, count):
    value = ref[pl.ds(start, count), 0:64]
    return jnp.concatenate([value[:, k * 8:(k + 1) * 8].reshape(count * 128, 128) for k in range(8)], axis=1)


def keys_of(tag):
    tag = tag.astype(jnp.float32)
    low = tag[0:1] * 32768.0
    return low, low + tag[1:2] * 256.0 + tag[2:3]


def kernel(emb_ref, cid_ref, ord_ref, out_ref, C, R, keycol, qk, acc, res, send_sems, fsem, zsem, bsem, rsem):
    x = lax.axis_index("grp")
    blk = lax.axis_index("blk")
    core = lax.rem(blk, 2)
    y = lax.rem(lax.div(blk, 2), NY)
    z = lax.div(blk, 2 * NY)

    def dev(dx, dy, dz, dc):
        cc = lax.rem(core + dc, 2)
        return (lax.rem(x + dx, NX), (lax.rem(z + dz, NZ) * NY + lax.rem(y + dy, NY)) * 2 + cc)

    def first(d):
        d = d % 4
        return dev((1 - core) * d, core * d, 0, 0)

    def second(d):
        d = d % 4
        return dev(core * d, (1 - core) * d, 0, 0)

    def zdev(d):
        return dev(0, 0, d % NZ, 0)

    sib = dev(0, 0, 0, 1)

    barrier = pltpu.get_barrier_semaphore()
    for t in (first(1), first(-1), second(1), second(-1), zdev(1), zdev(-1), sib):
        pl.semaphore_signal(barrier, inc=1, device_id=t, device_id_type=MESH)

    values = emb_ref[...].astype(jnp.float32)
    total = jnp.sum(values * values, axis=1, keepdims=True)
    unit = (values * lax.rsqrt(total + 1e-06)).astype(jnp.bfloat16)
    for k in range(8):
        piece = unit[:, k * 128:(k + 1) * 128].reshape(8, 16, 128)
        C[0, k * 8:(k + 1) * 8] = piece
        R[0, k * 8:(k + 1) * 8] = piece
    row = lax.broadcasted_iota(jnp.int32, (16, 128), 0)
    order = ord_ref[...]
    tag = jnp.where(row == 0, cid_ref[...], jnp.where(row == 1, lax.shift_right_logical(order, 8), jnp.where(row == 2, order & 255, 0)))
    tag = tag.astype(jnp.float32).astype(jnp.bfloat16)
    C[0, 64] = tag
    R[0, 64] = tag
    pl.semaphore_wait(barrier, 7)

    sends = []

    def send(src, dst, sem, target):
        d = pltpu.make_async_remote_copy(src_ref=src, dst_ref=dst, send_sem=send_sems.at[len(sends)], recv_sem=sem, device_id=target, device_id_type=MESH)
        d.start()
        sends.append(d)

    def cpart(i, h):
        return C.at[i, pl.ds(*HALF[h])]

    def rpart(i, h):
        return R.at[i, pl.ds(*HALF[h])]

    def send_c(a, b, h, target):
        i, j = slot_c(*a), slot_c(*b)
        send(cpart(i, h), cpart(j, h), fsem.at[j, h], target)

    def wait_c(a, h):
        j = slot_c(*a)
        pltpu.make_async_remote_copy(src_ref=cpart(j, h), dst_ref=cpart(j, h), send_sem=send_sems.at[0], recv_sem=fsem.at[j, h], device_id=sib, device_id_type=MESH).wait_recv()

    def send_z(i, j, h, d):
        i, j = 2 * ZOFF.index(i), 2 * ZOFF.index(j)
        send(rpart(i, h), rpart(j, h), zsem.at[j // 2, h], zdev(d))

    def wait_z(k, h):
        j = 2 * ZOFF.index(k)
        pltpu.make_async_remote_copy(src_ref=rpart(j, h), dst_ref=rpart(j, h), send_sem=send_sems.at[0], recv_sem=zsem.at[j // 2, h], device_id=sib, device_id_type=MESH).wait_recv()

    def send_sib(k):
        j = 2 * ZOFF.index(k)
        send(R.at[j], R.at[j + 1], bsem.at[j // 2], sib)

    def wait_sib(k):
        j = 2 * ZOFF.index(k)
        pltpu.make_async_remote_copy(src_ref=R.at[j + 1], dst_ref=R.at[j + 1], send_sem=send_sems.at[0], recv_sem=bsem.at[j // 2], device_id=sib, device_id_type=MESH).wait_recv()

    def line(a, h):
        send_c((a, 0), (a, -1), h, second(1))
        send_c((a, 0), (a, 1), h, second(-1))

    def got_f(a, h):
        wait_c((a, 0), h)
        if (a, h) == (-1, 0):
            send_c((-1, 0), (2, 0), 0, first(1))
        if (a, h) == (1, 1):
            send_c((1, 0), (2, 0), 1, first(-1))
        line(a, h)

    def got_s(a, b, h):
        wait_c((a, b), h)
        if (b, h) == (-1, 0):
            send_c((a, -1), (a, 2), 0, second(1))
        if (b, h) == (1, 1):
            send_c((a, 1), (a, 2), 1, second(-1))

    def got_z(k, h):
        wait_z(k, h)
        if k < 0 and (k > -3 or h == 0):
            send_z(k, k - 1 if k > -3 else 4, h, 1)
        if 0 < k < 4 and (k < 3 or h == 1):
            send_z(k, k + 1, h, -1)

    def ready_r(k):
        wait_sib(k)
        u = ZOFF.index(k)
        for c in range(2):
            low, high = keys_of(R[2 * u + c, 64])
            qk[u, 0:1, c * 128:(c + 1) * 128] = low
            qk[u, 1:2, c * 128:(c + 1) * 128] = high

    def ready_c(start, count):
        def one(j, carry):
            _, high = keys_of(C[j, 64])
            keycol[j] = jnp.broadcast_to(high, (128, 128)).T
            return carry

        lax.fori_loop(start, start + count, one, 0)

    def compute(start, count, u0, u1):
        def one(u, carry):
            scores = lax.dot_general(
                wide(C, start, count), wide(R, 2 * u, 2), (((1,), (1,)), ((), ())),
                preferred_element_type=jnp.float32,
            )
            column = keycol[pl.ds(start, count)].reshape(count * 128, 128)
            column = jnp.concatenate([column, column], axis=1)
            mask = (column >= qk[u, 0:1, :]) & (column < qk[u, 1:2, :])
            kept = jnp.where(mask, scores, jnp.float32(-1.0))
            best = jnp.max(kept.reshape(count * 16, 8, 256), axis=0)
            acc[2 * u] = jnp.maximum(acc[2 * u], best[:, 0:128])
            acc[2 * u + 1] = jnp.maximum(acc[2 * u + 1], best[:, 128:256])
            return carry

        lax.fori_loop(u0, u1, one, 0)

    send_c((0, 0), (-1, 0), 0, first(1))
    send_c((0, 0), (1, 0), 1, first(-1))
    send_z(0, -1, 0, 1)
    send_z(0, 1, 1, -1)
    send_c((0, 0), (-1, 0), 1, first(1))
    send_c((0, 0), (1, 0), 0, first(-1))
    send_z(0, -1, 1, 1)
    send_z(0, 1, 0, -1)
    send_sib(0)
    acc[...] = jnp.full(acc.shape, -1.0, jnp.float32)
    sends[0].wait_send()
    sends[1].wait_send()
    line(0, 0)
    line(0, 1)

    got_f(-1, 0); got_f(1, 1)
    got_f(-1, 1); got_f(1, 0)
    got_z(-1, 0); got_z(1, 1)
    got_s(0, -1, 0); got_s(0, 1, 1)
    got_z(-1, 1); got_z(1, 0)
    send_sib(-1); send_sib(1)
    got_f(2, 0); got_f(2, 1)
    got_s(0, -1, 1); got_s(0, 1, 0)
    got_s(-1, -1, 0); got_s(-1, 1, 1)
    got_s(-1, -1, 1); got_s(-1, 1, 0)
    got_z(-2, 0); got_z(2, 1)
    got_s(0, 2, 0); got_s(0, 2, 1)
    ready_r(0); ready_r(-1); ready_r(1)
    ready_c(0, 4)
    compute(0, 4, 0, 3)
    got_s(1, -1, 0); got_s(1, 1, 1)
    got_s(1, -1, 1); got_s(1, 1, 0)
    got_z(-2, 1); got_z(2, 0)
    send_sib(-2); send_sib(2)
    got_s(-1, 2, 0); got_s(-1, 2, 1)
    ready_c(4, 4)
    compute(4, 4, 0, 3)
    got_z(-3, 0); got_z(3, 1)
    got_s(2, -1, 0); got_s(2, 1, 1)
    got_s(1, 2, 0); got_s(1, 2, 1)
    ready_r(-2); ready_r(2)
    compute(0, 8, 3, 5)
    got_z(-3, 1); got_z(3, 0)
    send_sib(-3); send_sib(3)
    ready_c(8, 4)
    compute(8, 4, 0, 5)
    got_s(2, -1, 1); got_s(2, 1, 0)
    ready_r(-3); ready_r(3)
    compute(0, 12, 5, 7)
    got_z(4, 0); got_z(4, 1)
    send_sib(4)
    got_s(2, 2, 0); got_s(2, 2, 1)
    ready_c(12, 4)
    compute(12, 4, 0, 7)
    ready_r(4)
    compute(0, 16, 7, 8)

    waits = []
    for k in ZOFF:
        for c in range(2):
            if (k, c) == (0, 0):
                continue
            i = 2 * ZOFF.index(k) + c
            j = 2 * ZOFF.index(-k if k != 4 else 4) + c
            d = pltpu.make_async_remote_copy(
                src_ref=acc.at[i], dst_ref=res.at[j], send_sem=send_sems.at[len(sends)], recv_sem=rsem.at[j],
                device_id=dev(0, 0, k % NZ, c), device_id_type=MESH,
            )
            d.start()
            sends.append(d)
            waits.append(j)
    for d in sends[2:]:
        d.wait_send()
    best = acc[0]
    for j in waits:
        pltpu.make_async_remote_copy(
            src_ref=res.at[j], dst_ref=res.at[j], send_sem=send_sems.at[0], recv_sem=rsem.at[j],
            device_id=sib, device_id_type=MESH,
        ).wait_recv()
        best = jnp.maximum(best, res[j])
    out_ref[...] = jnp.max(best, axis=0, keepdims=True)


def shards(embeddings, cluster_ids, row_order):
    out = pl.pallas_call(
        kernel,
        out_shape=jax.ShapeDtypeStruct((1, 128), jnp.float32),
        in_specs=[pl.BlockSpec(memory_space=pltpu.VMEM)] * 3,
        out_specs=pl.BlockSpec(memory_space=pltpu.VMEM),
        scratch_shapes=[
            pltpu.VMEM((16, CHUNKS, 16, 128), jnp.bfloat16),
            pltpu.VMEM((16, CHUNKS, 16, 128), jnp.bfloat16),
            pltpu.VMEM((16, 128, 128), jnp.float32),
            pltpu.VMEM((8, 8, 256), jnp.float32),
            pltpu.VMEM((16, 8, 128), jnp.float32),
            pltpu.VMEM((16, 8, 128), jnp.float32),
            pltpu.SemaphoreType.DMA((96,)),
            pltpu.SemaphoreType.DMA((16, 2)),
            pltpu.SemaphoreType.DMA((8, 2)),
            pltpu.SemaphoreType.DMA((8,)),
            pltpu.SemaphoreType.DMA((16,)),
        ],
        compiler_params=pltpu.CompilerParams(collective_id=0, has_side_effects=True, vmem_limit_bytes=48 << 20),
        name="gather_all",
    )(embeddings, cluster_ids.reshape(1, 128), row_order.reshape(1, 128))
    return out.reshape(128)


def solution(mesh):
    in_specs = (P(("grp", "blk"), None), P(("grp", "blk")), P(("grp", "blk")))
    return jax.shard_map(shards, mesh=mesh, in_specs=in_specs, out_specs=P(("grp", "blk")), check_vma=False)
```

```python
import functools
import jax
import jax.numpy as jnp
from jax import lax
from jax.experimental import pallas as pl
from jax.experimental.pallas import tpu as pltpu
from jax.sharding import PartitionSpec as P

MESH = pl.DeviceIdType.MESH
NX, NY, NZ = 4, 4, 8
CHUNKS = 65
HALVES = ((0, 32), (32, 33))
QUARTERS = ((0, 16), (16, 16), (32, 16), (48, 17))
PLANE = ((0, 0), (1, 0), (0, 1), (3, 3), (2, 0), (0, 2), (2, 3), (3, 2), (1, 3), (2, 2))
COLUMN = (0, -1, 1, -2, 2, -3, 3, 4)

def wide(ref, start, count):
    value = ref[pl.ds(start, count), 0:64]
    return jnp.concatenate([value[:, k * 8:(k + 1) * 8].reshape(count * 128, 128) for k in range(8)], axis=1)


def keys_of(tag):
    tag = tag.astype(jnp.float32)
    low = tag[0:1] * 32768.0
    return low, low + tag[1:2] * 256.0 + tag[2:3]


def kernel(emb_ref, cid_ref, ord_ref, out_ref, C, R, keycol, qk, acc_r, acc_c, out_c, res_r, res_c, send_sems, csem, zsem, bsem, rsem_r, rsem_c):
    x = lax.axis_index("grp")
    blk = lax.axis_index("blk")
    core = lax.rem(blk, 2)
    y = lax.rem(lax.div(blk, 2), NY)
    z = lax.div(blk, 2 * NY)

    def dev(dx, dy, dz, dc):
        other = lax.rem(core + dc, 2)
        return (lax.rem(x + dx % NX, NX), (lax.rem(z + dz % NZ, NZ) * NY + lax.rem(y + dy % NY, NY)) * 2 + other)

    sib = dev(0, 0, 0, 1)

    barrier = pltpu.get_barrier_semaphore()
    near = [dev(1, 0, 0, 0), dev(-1, 0, 0, 0), dev(0, 1, 0, 0), dev(0, -1, 0, 0), dev(1, 1, 0, 0), dev(-1, -1, 0, 0), dev(0, 0, 1, 0), dev(0, 0, -1, 0), sib]
    for target in near:
        pl.semaphore_signal(barrier, inc=1, device_id=target, device_id_type=MESH)

    values = emb_ref[...].astype(jnp.float32)
    total = jnp.sum(values * values, axis=1, keepdims=True)
    unit = (values * lax.rsqrt(total + 1e-06)).astype(jnp.bfloat16)
    for k in range(8):
        piece = unit[:, k * 128:(k + 1) * 128].reshape(8, 16, 128)
        C[0, k * 8:(k + 1) * 8] = piece
        R[0, k * 8:(k + 1) * 8] = piece
    row = lax.broadcasted_iota(jnp.int32, (16, 128), 0)
    order = ord_ref[...]
    tag = jnp.where(row == 0, cid_ref[...], jnp.where(row == 1, lax.shift_right_logical(order, 8), jnp.where(row == 2, order & 255, 0)))
    tag = tag.astype(jnp.float32).astype(jnp.bfloat16)
    C[0, 64] = tag
    R[0, 64] = tag
    pl.semaphore_wait(barrier, len(near))

    sends = []

    def copy(src, dst, sem, target):
        d = pltpu.make_async_remote_copy(
            src_ref=src, dst_ref=dst, send_sem=send_sems.at[len(sends)], recv_sem=sem, device_id=target, device_id_type=MESH
        )
        d.start()
        sends.append(d)

    def arrived(dst, sem):
        pltpu.make_async_remote_copy(
            src_ref=dst, dst_ref=dst, send_sem=send_sems.at[0], recv_sem=sem, device_id=sib, device_id_type=MESH
        ).wait_recv()

    def cpart(j, h):
        return C.at[j, pl.ds(*HALVES[h])]

    def zpart(u, q):
        return R.at[2 * u, pl.ds(*QUARTERS[q])]

    def pass_c(d, step, h):
        i = PLANE.index(d)
        j = PLANE.index(((d[0] - step[0]) % NX, (d[1] - step[1]) % NY))
        copy(cpart(i, h), cpart(j, h), csem.at[j, h], dev(step[0], step[1], 0, 0))

    def got_c(d, h):
        j = PLANE.index(d)
        arrived(cpart(j, h), csem.at[j, h])

    def pass_z(k, q, steps=(1, -1)):
        i = COLUMN.index(k)
        for step in steps:
            if k * step > 0 or k == 4 or (abs(k) == 3 and q // 2 != (step + 1) // 2):
                continue
            to = k - step
            j = COLUMN.index(4 if abs(to) == 4 else to)
            copy(zpart(i, q), zpart(j, q), zsem.at[j, q], dev(0, 0, step, 0))

    def got_z(k, q):
        j = COLUMN.index(k)
        arrived(zpart(j, q), zsem.at[j, q])
        if k != 4:
            pass_z(k, q)

    def step_z(k, n):
        got_z(-k, (n + 2) % 4)
        got_z(k, n)

    def share(k):
        u = COLUMN.index(k)
        copy(R.at[2 * u], R.at[2 * u + 1], bsem.at[u], sib)

    def ready_r(k):
        u = COLUMN.index(k)
        arrived(R.at[2 * u + 1], bsem.at[u])
        for c in range(2):
            low, high = keys_of(R[2 * u + c, 64])
            qk[u, 0:1, c * 128:(c + 1) * 128] = low
            qk[u, 1:2, c * 128:(c + 1) * 128] = high

    def ready_c(start, count):
        def one(j, carry):
            _, high = keys_of(C[j, 64])
            keycol[j] = jnp.broadcast_to(high, (128, 128)).T
            return carry

        lax.fori_loop(start, start + count, one, 0)

    def compute(start, count, u0, u1):
        def one(u, carry):
            scores = lax.dot_general(
                wide(C, start, count), wide(R, 2 * u, 2), (((1,), (1,)), ((), ())),
                preferred_element_type=jnp.float32,
            )
            column = keycol[pl.ds(start, count)].reshape(count * 128, 128)
            column = jnp.concatenate([column, column], axis=1)
            low = qk[u, 0:1, :]
            high = qk[u, 1:2, :]
            low_r = jnp.where((column >= low) & (column < high), scores, jnp.float32(-1.0))
            best = jnp.max(low_r.reshape(count * 16, 8, 256), axis=0)
            acc_r[2 * u] = jnp.maximum(acc_r[2 * u], best[:, 0:128])
            acc_r[2 * u + 1] = jnp.maximum(acc_r[2 * u + 1], best[:, 128:256])
            low_c = jnp.where((column > high) & (column < low + 32768.0), scores, jnp.float32(-1.0))
            side = jnp.maximum(low_c[:, 0:128], low_c[:, 128:256]).reshape(count, 128, 128)
            acc_c[pl.ds(start, count)] = jnp.maximum(acc_c[pl.ds(start, count)], side)
            return carry

        if u1 - u0 == 1:
            one(u0, 0)
        else:
            lax.fori_loop(u0, u1, one, 0)

    def answer_r(k):
        u = COLUMN.index(k)
        v = COLUMN.index(4 if k == 4 else -k)
        for c in range(2):
            if (k, c) != (0, 0):
                copy(acc_r.at[2 * u + c], res_r.at[2 * v + c], rsem_r.at[2 * v + c], dev(0, 0, k, c))

    for q in range(4):
        pass_z(0, (q + 2) % 4, (1,))
        pass_z(0, q, (-1,))
        if q % 2 == 0:
            h = q // 2
            pass_c((0, 0), (-1, 0), h)
            pass_c((0, 0), (0, -1), h)
            pass_c((0, 0), (1, 1), 1 - h)
    share(0)
    acc_r[...] = jnp.full(acc_r.shape, -1.0, jnp.float32)
    acc_c[...] = jnp.full(acc_c.shape, -1.0, jnp.float32)

    step_z(1, 0)
    step_z(1, 1)
    got_c((1, 0), 0)
    pass_c((1, 0), (-1, 0), 0)
    got_c((0, 1), 0)
    pass_c((0, 1), (0, -1), 0)
    got_c((3, 3), 1)
    pass_c((3, 3), (1, 0), 1)
    pass_c((3, 3), (0, 1), 1)
    step_z(1, 2)
    pass_c((1, 0), (0, 1), 0)
    step_z(1, 3)
    share(-1)
    share(1)
    got_c((1, 0), 1)
    pass_c((1, 0), (-1, 0), 1)
    got_c((0, 1), 1)
    pass_c((0, 1), (0, -1), 1)
    got_c((3, 3), 0)
    pass_c((3, 3), (1, 0), 0)
    pass_c((3, 3), (0, 1), 0)
    ready_r(0)
    ready_c(0, 4)
    step_z(2, 0)
    compute(0, 4, 0, 1)
    ready_r(-1)
    ready_r(1)
    step_z(2, 1)
    got_c((2, 3), 1)
    pass_c((2, 3), (1, 0), 1)
    got_c((3, 2), 1)
    pass_c((3, 2), (1, 0), 1)
    compute(0, 4, 1, 3)
    step_z(2, 2)
    step_z(2, 3)
    share(-2)
    share(2)
    got_c((2, 3), 0)
    pass_c((2, 3), (0, 1), 0)
    got_c((2, 0), 0)
    got_c((2, 0), 1)
    got_c((0, 2), 0)
    got_c((0, 2), 1)
    got_c((3, 2), 0)
    ready_c(4, 4)
    compute(4, 4, 0, 1)
    step_z(3, 0)
    compute(4, 4, 1, 3)
    step_z(3, 1)
    ready_r(-2)
    ready_r(2)
    compute(0, 8, 3, 4)
    step_z(3, 2)
    compute(0, 8, 4, 5)
    step_z(3, 3)
    share(-3)
    share(3)
    got_c((1, 3), 0)
    got_c((1, 3), 1)
    got_c((2, 2), 0)
    got_c((2, 2), 1)
    ready_c(8, 2)
    compute(8, 2, 0, 5)
    for k in (0, -1, 1, -2, 2):
        answer_r(k)
    for q in range(4):
        got_z(4, q)
    share(4)
    ready_r(-3)
    ready_r(3)
    compute(0, 10, 5, 7)
    answer_r(-3)
    answer_r(3)
    ready_r(4)
    compute(0, 10, 7, 8)
    answer_r(4)
    for j, d in enumerate(PLANE):
        out_c[j] = jnp.max(acc_c[j].T.reshape(16, 8, 128), axis=0)
        if j:
            copy(out_c.at[j], res_c.at[j], rsem_c.at[j], dev(d[0], d[1], 0, 0))

    best = jnp.maximum(acc_r[0], out_c[0])
    for j in range(1, 16):
        arrived(res_r.at[j], rsem_r.at[j])
        best = jnp.maximum(best, res_r[j])
    for j in range(1, 10):
        arrived(res_c.at[j], rsem_c.at[j])
        best = jnp.maximum(best, res_c[j])
    out_ref[...] = jnp.max(best, axis=0, keepdims=True)
    for d in sends:
        d.wait_send()


def shards(embeddings, cluster_ids, row_order):
    out = pl.pallas_call(
        kernel,
        out_shape=jax.ShapeDtypeStruct((1, 128), jnp.float32),
        in_specs=[pl.BlockSpec(memory_space=pltpu.VMEM)] * 3,
        out_specs=pl.BlockSpec(memory_space=pltpu.VMEM),
        scratch_shapes=[
            pltpu.VMEM((10, CHUNKS, 16, 128), jnp.bfloat16),
            pltpu.VMEM((16, CHUNKS, 16, 128), jnp.bfloat16),
            pltpu.VMEM((10, 128, 128), jnp.float32),
            pltpu.VMEM((8, 8, 256), jnp.float32),
            pltpu.VMEM((16, 8, 128), jnp.float32),
            pltpu.VMEM((10, 128, 128), jnp.float32),
            pltpu.VMEM((10, 8, 128), jnp.float32),
            pltpu.VMEM((16, 8, 128), jnp.float32),
            pltpu.VMEM((10, 8, 128), jnp.float32),
            pltpu.SemaphoreType.DMA((96,)),
            pltpu.SemaphoreType.DMA((10, 2)),
            pltpu.SemaphoreType.DMA((8, 4)),
            pltpu.SemaphoreType.DMA((8,)),
            pltpu.SemaphoreType.DMA((16,)),
            pltpu.SemaphoreType.DMA((10,)),
        ],
        compiler_params=pltpu.CompilerParams(collective_id=0, has_side_effects=True, vmem_limit_bytes=48 << 20),
        name="nearest_earlier",
    )(embeddings, cluster_ids.reshape(1, 128), row_order.reshape(1, 128))
    return out.reshape(128)


def solution(mesh):
    in_specs = (P(("grp", "blk"), None), P(("grp", "blk")), P(("grp", "blk")))
    return jax.shard_map(shards, mesh=mesh, in_specs=in_specs, out_specs=P(("grp", "blk")), check_vma=False)
```

```python
import jax
import jax.numpy as jnp
from jax import lax
from jax.experimental import pallas as pl
from jax.experimental.pallas import tpu as pltpu
from jax.sharding import PartitionSpec as P

MESH = pl.DeviceIdType.MESH
NX, NY, NZ = 4, 4, 8
CHUNKS = 65
HALVES = ((0, 33), (33, 32))
QUARTERS = ((0, 17), (17, 16), (33, 16), (49, 16))
EARLY, LATE = (0, 1, 4, 5), (2, 3, 6, 7)
PLANE = ((1, 0), (0, 1), (3, 3), (2, 3), (1, 3), (3, 2), (0, 0), (2, 0), (0, 2), (2, 2))
OWN = PLANE.index((0, 0))
COLUMN = (0, 1, -1, 2, -2, 3, -3, 4)
ONWARD = {
    (0, 0): (((-1, 0), (0, 1, 2, 3)), ((0, -1), (0, 1, 2, 3))),
    (1, 0): (((-1, 0), (0, 1, 2, 3)), ((0, 1), (0, 1))),
    (0, 1): (((0, -1), (0, 1, 2, 3)),),
    (3, 3): (((1, 0), (0, 1, 2, 3)), ((0, 1), (0, 1, 2, 3))),
    (2, 3): (((1, 0), (2, 3)), ((0, 1), (0, 1))),
    (3, 2): (((1, 0), (2, 3)),),
}


def wide(ref, start, count, features=range(8)):
    return jnp.concatenate(
        [ref[pl.ds(start, count), 1 + k * 8:9 + k * 8].reshape(count * 128, 128) for k in features], axis=1
    )


def product(left, right):
    return lax.dot_general(left, right, (((1,), (1,)), ((), ())), preferred_element_type=jnp.float32)


def keys_of(tag):
    tag = tag.astype(jnp.float32)
    low = tag[0:1] * 32768.0
    return low, low + tag[1:2] * 256.0 + tag[2:3]


def kernel(emb_hbm, cid_hbm, ord_hbm, out_ref, emb_ref, cid_ref, ord_ref, in_sems, C, R, row_key, low_key, high_key, half, acc_r, acc_c, out_r, res_r, res_c, send_sems, csem, ssem, zsem, rsem_r, rsem_c, corner_sem):
    loads = [
        pltpu.make_async_copy(src, dst, in_sems.at[i])
        for i, (src, dst) in enumerate(((emb_hbm, emb_ref), (cid_hbm, cid_ref), (ord_hbm, ord_ref)))
    ]
    for load in loads:
        load.start()
    x = lax.axis_index("grp")
    blk = lax.axis_index("blk")
    core = lax.rem(blk, 2)
    y = lax.rem(lax.div(blk, 2), NY)
    z = lax.div(blk, 2 * NY)

    def dev(dx, dy, dz, dc):
        other = lax.rem(core + dc, 2)
        return (lax.rem(x + dx % NX, NX), (lax.rem(z + dz % NZ, NZ) * NY + lax.rem(y + dy % NY, NY)) * 2 + other)

    sib = dev(0, 0, 0, 1)

    barrier = pltpu.get_barrier_semaphore()
    near = [dev(1, 0, 0, 0), dev(-1, 0, 0, 0), dev(0, 1, 0, 0), dev(0, -1, 0, 0), dev(0, 0, 1, 0), dev(0, 0, -1, 0), sib]
    for target in near:
        pl.semaphore_signal(barrier, inc=1, device_id=target, device_id_type=MESH)

    for load in loads:
        load.wait()
    values = emb_ref[...].astype(jnp.float32)
    total = jnp.sum(values * values, axis=1, keepdims=True)
    unit = (values * lax.rsqrt(total + 1e-06)).astype(jnp.bfloat16)
    for k in range(8):
        piece = unit[:, k * 128:(k + 1) * 128].reshape(8, 16, 128)
        C[2 * OWN, 1 + k * 8:9 + k * 8] = piece
        R[0, 1 + k * 8:9 + k * 8] = piece
    row = lax.broadcasted_iota(jnp.int32, (16, 128), 0)
    order = ord_ref[...]
    tag = jnp.where(row == 0, cid_ref[...], jnp.where(row == 1, lax.shift_right_logical(order, 8), jnp.where(row == 2, order & 255, 0)))
    tag = tag.astype(jnp.float32).astype(jnp.bfloat16)
    C[2 * OWN, 0] = tag
    R[0, 0] = tag
    pl.semaphore_wait(barrier, len(near))

    sends = []

    def copy(src, dst, sem, target):
        d = pltpu.make_async_remote_copy(
            src_ref=src, dst_ref=dst, send_sem=send_sems.at[len(sends)], recv_sem=sem, device_id=target, device_id_type=MESH
        )
        d.start()
        sends.append(d)

    def arrived(dst, sem):
        pltpu.make_async_remote_copy(
            src_ref=dst, dst_ref=dst, send_sem=send_sems.at[0], recv_sem=sem, device_id=sib, device_id_type=MESH
        ).wait_recv()

    def cpart(i, q):
        return C.at[2 * i, pl.ds(*QUARTERS[q])]

    def zpart(u, q):
        return R.at[u, pl.ds(*QUARTERS[q])]

    def pass_c(d, step, q):
        i = PLANE.index(d)
        j = PLANE.index(((d[0] - step[0]) % NX, (d[1] - step[1]) % NY))
        copy(cpart(i, q), cpart(j, q), csem.at[j, q], dev(step[0], step[1], 0, 0))

    def share(i, h):
        copy(C.at[2 * i, pl.ds(*HALVES[h])], C.at[2 * i + 1, pl.ds(*HALVES[h])], ssem.at[i, h], sib)

    def got_c(d, *quarters):
        i = PLANE.index(d)
        for q in quarters:
            arrived(cpart(i, q), csem.at[i, q])
            for step, some in ONWARD.get(d, ()):
                if q in some:
                    pass_c(d, step, q)
            if q % 2:
                share(i, q // 2)

    def pass_z(k, q, steps=(1, -1)):
        i = COLUMN.index(k)
        for step in steps:
            if k * step > 0 or (abs(k) == 3 and q // 2 != (step + 1) // 2):
                continue
            to = k - step
            j = COLUMN.index(4 if abs(to) == 4 else to)
            copy(zpart(i, q), zpart(j, q), zsem.at[j, q], dev(0, 0, step, 0))

    def got_z(k, q):
        j = COLUMN.index(k)
        arrived(zpart(j, q), zsem.at[j, q])
        if k != 4:
            pass_z(k, q)

    def step_z(k, n):
        got_z(-k, (n + 2) % 4)
        got_z(k, n)

    def ready_c(start, count):
        for i in range(start, start + count):
            for h in range(2):
                arrived(C.at[2 * i + 1, pl.ds(*HALVES[h])], ssem.at[i, h])
            for j in (2 * i, 2 * i + 1):
                low, high = keys_of(C[j, 0])
                low_key[j, 0:1, :] = low
                high_key[j, 0:1, :] = high

    def ready_r(*ks):
        for k in ks:
            u = COLUMN.index(k)
            _, high = keys_of(R[u, 0])
            row_key[u] = jnp.broadcast_to(high, (128, 128)).T

    def use(scores, start, count, ks):
        for a, k in enumerate(ks):
            u = COLUMN.index(k)
            key = row_key[u]
            side = acc_r[u]
            for b in range(2 * count):
                j = 2 * start + b
                part = scores[a * 128:(a + 1) * 128, b * 128:(b + 1) * 128]
                low = low_key[j, 0:1, :]
                high = high_key[j, 0:1, :]
                earlier = jnp.where((key >= low) & (key < high), part, jnp.float32(-1.0))
                acc_c[j] = jnp.maximum(acc_c[j], jnp.max(earlier.reshape(16, 8, 128), axis=0))
                side = jnp.maximum(side, jnp.where((key > high) & (key < low + 32768.0), part, jnp.float32(-1.0)))
            acc_r[u] = side

    def compute(start, count, *ks):
        rows = jnp.concatenate([wide(R, COLUMN.index(k), 1) for k in ks], axis=0)
        use(product(rows, wide(C, 2 * start, 2 * count)), start, count, ks)

    def answer_r(*ks):
        for k in ks:
            u = COLUMN.index(k)
            out_r[u] = jnp.max(acc_r[u].T.reshape(16, 8, 128), axis=0)
            if k:
                v = COLUMN.index(4 if k == 4 else -k)
                copy(out_r.at[u], res_r.at[v], rsem_r.at[v], dev(0, 0, k, 0))

    def answer_c(*blocks):
        for i in blocks:
            for c in range(2):
                j = 2 * i + c
                if j != 2 * OWN:
                    copy(acc_c.at[j], res_c.at[j], rsem_c.at[j], dev(PLANE[i][0], PLANE[i][1], 0, c))

    pl.semaphore_signal(corner_sem, inc=1, device_id=dev(-1, 0, 0, 0), device_id_type=MESH)

    for q in range(4):
        pass_z(0, (q + 2) % 4, (1,))
        pass_z(0, q, (-1,))
        for step, _ in ONWARD[(0, 0)]:
            pass_c((0, 0), step, q)
    share(OWN, 0)
    share(OWN, 1)
    acc_r[...] = jnp.full(acc_r.shape, -1.0, jnp.float32)
    acc_c[...] = jnp.full(acc_c.shape, -1.0, jnp.float32)
    pl.semaphore_wait(corner_sem, 1)
    for q in (2, 3, 0, 1):
        pass_c((0, 0), (1, 1), q)

    step_z(1, 0)
    got_c((1, 0), 0)
    got_c((0, 1), 0)
    step_z(1, 1)
    got_c((1, 0), 1)
    got_c((0, 1), 1)
    got_c((3, 3), 2)
    step_z(1, 2)
    got_c((1, 0), 2)
    got_c((0, 1), 2)
    got_c((3, 3), 3)
    step_z(1, 3)
    got_c((1, 0), 3)
    got_c((0, 1), 3)
    got_c((3, 3), 0)
    ready_r(0, 1, -1)
    ready_c(OWN, 1)
    compute(6, 1, 0, 1)
    step_z(2, 0)
    got_c((2, 0), 0)
    got_c((0, 2), 0)
    got_c((3, 3), 1)
    ready_c(0, 2)
    compute(0, 2, 0, 1, -1)
    step_z(2, 1)
    got_c((2, 0), 1)
    got_c((0, 2), 1)
    got_c((2, 3), 2)
    got_c((1, 3), 0)
    step_z(2, 2)
    got_c((2, 3), 3)
    got_c((1, 3), 1)
    got_c((2, 0), 2)
    got_c((0, 2), 2)
    got_c((3, 2), 2)
    got_c((2, 3), 0)
    step_z(2, 3)
    got_c((2, 0), 3)
    got_c((0, 2), 3)
    ready_r(2, -2)
    compute(0, 2, 2, -2)
    got_c((3, 2), 3)
    got_c((2, 3), 1)
    step_z(3, 0)
    ready_c(7, 2)
    compute(7, 2, 0, 1, 2)
    got_c((3, 2), 0)
    got_c((1, 3), 2)
    step_z(3, 1)
    ready_c(2, 2)
    compute(2, 2, 0, 1, -1)
    got_c((3, 2), 1)
    got_c((1, 3), 3)
    step_z(3, 2)
    compute(2, 2, 2, -2)
    got_c((2, 2), 2, 0)
    step_z(3, 3)
    ready_c(4, 2)
    compute(4, 2, 0, 1, -1, 2, -2)
    got_c((2, 2), 3, 1)
    ready_r(3, -3)
    compute(0, 6, 3, -3)
    answer_r(-1, -2)
    compute(6, 3, 3)
    compute(6, 1, 2)
    got_z(4, 2)
    got_z(4, 0)
    ready_r(4)
    ready_c(9, 1)
    half[...] = product(wide(R, 7, 1, EARLY), wide(C, 0, 20, EARLY))
    compute(9, 1, 0, 1, 2, 3)
    answer_r(-3)
    got_z(4, 3)
    got_z(4, 1)
    use(half[...] + product(wide(R, 7, 1, LATE), wide(C, 0, 20, LATE)), 0, 10, (4,))
    answer_r(4)
    answer_c(9, 3, 5, 4, 7, 8, 2, 0, 1, 6)
    answer_r(3, 2, 1, 0)

    for d in sends:
        d.wait_send()
    best = jnp.maximum(out_r[0], acc_c[2 * OWN])
    for u in range(1, 8):
        arrived(res_r.at[u], rsem_r.at[u])
        best = jnp.maximum(best, res_r[u])
    for j in range(20):
        if j != 2 * OWN:
            arrived(res_c.at[j], rsem_c.at[j])
            best = jnp.maximum(best, res_c[j])
    out_ref[...] = jnp.max(best, axis=0, keepdims=True)


def shards(embeddings, cluster_ids, row_order):
    out = pl.pallas_call(
        kernel,
        out_shape=jax.ShapeDtypeStruct((1, 128), jnp.float32),
        in_specs=[pl.BlockSpec(memory_space=pltpu.HBM)] * 3,
        out_specs=pl.BlockSpec(memory_space=pltpu.VMEM),
        scratch_shapes=[
            pltpu.VMEM((128, 1024), jnp.bfloat16),
            pltpu.VMEM((1, 128), jnp.int32),
            pltpu.VMEM((1, 128), jnp.int32),
            pltpu.SemaphoreType.DMA((3,)),
            pltpu.VMEM((20, CHUNKS, 16, 128), jnp.bfloat16),
            pltpu.VMEM((8, CHUNKS, 16, 128), jnp.bfloat16),
            pltpu.VMEM((8, 128, 128), jnp.float32),
            pltpu.VMEM((20, 8, 128), jnp.float32),
            pltpu.VMEM((20, 8, 128), jnp.float32),
            pltpu.VMEM((128, 2560), jnp.float32),
            pltpu.VMEM((8, 128, 128), jnp.float32),
            pltpu.VMEM((20, 8, 128), jnp.float32),
            pltpu.VMEM((8, 8, 128), jnp.float32),
            pltpu.VMEM((8, 8, 128), jnp.float32),
            pltpu.VMEM((20, 8, 128), jnp.float32),
            pltpu.SemaphoreType.DMA((128,)),
            pltpu.SemaphoreType.DMA((10, 4)),
            pltpu.SemaphoreType.DMA((10, 2)),
            pltpu.SemaphoreType.DMA((8, 4)),
            pltpu.SemaphoreType.DMA((8,)),
            pltpu.SemaphoreType.DMA((20,)),
            pltpu.SemaphoreType.REGULAR,
        ],
        compiler_params=pltpu.CompilerParams(collective_id=0, has_side_effects=True, vmem_limit_bytes=64 << 20),
        name="nearest_earlier",
    )(embeddings, cluster_ids.reshape(1, 128), row_order.reshape(1, 128))
    return out.reshape(128)


def solution(mesh):
    in_specs = (P(("grp", "blk"), None), P(("grp", "blk")), P(("grp", "blk")))
    return jax.shard_map(shards, mesh=mesh, in_specs=in_specs, out_specs=P(("grp", "blk")), check_vma=False)
```

```python
import jax
import jax.numpy as jnp
from jax import lax
from jax.experimental import pallas as pl
from jax.experimental.pallas import tpu as pltpu
from jax.sharding import PartitionSpec as P

MESH = pl.DeviceIdType.MESH
NX, NY, NZ = 4, 4, 8
CHUNKS = 65
HALVES = ((0, 33), (33, 32))
QUARTERS = ((0, 17), (17, 16), (33, 16), (49, 16))
EARLY, LATE = (0, 1, 4, 5), (2, 3, 6, 7)
PLANE = ((1, 0), (0, 1), (3, 3), (2, 3), (1, 3), (3, 2), (0, 0), (2, 0), (0, 2), (2, 2))
OWN = PLANE.index((0, 0))
COLUMN = (0, 1, -1, 2, -2, 3, -3, 4)
ONWARD = {
    (0, 0): (((-1, 0), (0, 1, 2, 3)), ((0, -1), (0, 1, 2, 3))),
    (1, 0): (((-1, 0), (0, 1, 2, 3)), ((0, 1), (0, 1))),
    (0, 1): (((0, -1), (0, 1, 2, 3)),),
    (3, 3): (((1, 0), (0, 1, 2, 3)), ((0, 1), (0, 1, 2, 3))),
    (2, 3): (((1, 0), (2, 3)), ((0, 1), (0, 1))),
    (3, 2): (((1, 0), (2, 3)),),
}


def rows_of(R, u, features=range(8)):
    return jnp.concatenate([R[u, 1 + k * 8:9 + k * 8].reshape(128, 128) for k in features], axis=1)


def columns_of(C, j, features=range(8)):
    return jnp.concatenate([C[j, 1 + k * 8:9 + k * 8].reshape(128, 128) for k in features], axis=0)


def product(rows, columns):
    return jnp.dot(rows, columns, preferred_element_type=jnp.float32)


def keys_of(tag):
    tag = tag.astype(jnp.float32)
    low = tag[0:1] * 32768.0
    return low, low + tag[1:2] * 256.0 + tag[2:3]


def kernel(emb_hbm, cid_hbm, ord_hbm, out_ref, emb_ref, cid_ref, ord_ref, in_sems, C, R, row_key, low_key, high_key, half, acc_r, acc_c, out_r, res_r, res_c, send_sems, csem, ssem, zsem, rsem_r, rsem_c, corner_sem):
    loads = [
        pltpu.make_async_copy(src, dst, in_sems.at[i])
        for i, (src, dst) in enumerate(((emb_hbm, emb_ref), (cid_hbm, cid_ref), (ord_hbm, ord_ref)))
    ]
    for load in loads:
        load.start()
    x = lax.axis_index("grp")
    blk = lax.axis_index("blk")
    core = lax.rem(blk, 2)
    y = lax.rem(lax.div(blk, 2), NY)
    z = lax.div(blk, 2 * NY)

    def dev(dx, dy, dz, dc):
        other = lax.rem(core + dc, 2)
        return (lax.rem(x + dx % NX, NX), (lax.rem(z + dz % NZ, NZ) * NY + lax.rem(y + dy % NY, NY)) * 2 + other)

    sib = dev(0, 0, 0, 1)

    barrier = pltpu.get_barrier_semaphore()
    near = [dev(1, 0, 0, 0), dev(-1, 0, 0, 0), dev(0, 1, 0, 0), dev(0, -1, 0, 0), dev(0, 0, 1, 0), dev(0, 0, -1, 0), sib]
    for target in near:
        pl.semaphore_signal(barrier, inc=1, device_id=target, device_id_type=MESH)

    for load in loads:
        load.wait()
    values = emb_ref[...].astype(jnp.float32)
    total = jnp.sum(values * values, axis=1, keepdims=True)
    unit = values * lax.rsqrt(total + 1e-06)
    for k in range(8):
        R[0, 1 + k * 8:9 + k * 8] = unit[:, k * 128:(k + 1) * 128].astype(jnp.bfloat16).reshape(8, 16, 128)
    row = lax.broadcasted_iota(jnp.int32, (16, 128), 0)
    order = ord_ref[...]
    tag = jnp.where(row == 0, cid_ref[...], jnp.where(row == 1, lax.shift_right_logical(order, 8), jnp.where(row == 2, order & 255, 0)))
    tag = tag.astype(jnp.float32).astype(jnp.bfloat16)
    C[2 * OWN, 0] = tag
    R[0, 0] = tag
    pl.semaphore_wait(barrier, len(near))

    sends = []

    def copy(src, dst, sem, target):
        d = pltpu.make_async_remote_copy(
            src_ref=src, dst_ref=dst, send_sem=send_sems.at[len(sends)], recv_sem=sem, device_id=target, device_id_type=MESH
        )
        d.start()
        sends.append(d)

    def arrived(dst, sem):
        pltpu.make_async_remote_copy(
            src_ref=dst, dst_ref=dst, send_sem=send_sems.at[0], recv_sem=sem, device_id=sib, device_id_type=MESH
        ).wait_recv()

    def cpart(i, q):
        return C.at[2 * i, pl.ds(*QUARTERS[q])]

    def zpart(u, q):
        return R.at[u, pl.ds(*QUARTERS[q])]

    def pass_c(d, step, q):
        i = PLANE.index(d)
        j = PLANE.index(((d[0] - step[0]) % NX, (d[1] - step[1]) % NY))
        copy(cpart(i, q), cpart(j, q), csem.at[j, q], dev(step[0], step[1], 0, 0))

    def share(i, h):
        copy(C.at[2 * i, pl.ds(*HALVES[h])], C.at[2 * i + 1, pl.ds(*HALVES[h])], ssem.at[i, h], sib)

    def got_c(d, *quarters):
        i = PLANE.index(d)
        for q in quarters:
            arrived(cpart(i, q), csem.at[i, q])
            for step, some in ONWARD.get(d, ()):
                if q in some:
                    pass_c(d, step, q)
            if q % 2:
                share(i, q // 2)

    def pass_z(k, q, steps=(1, -1)):
        i = COLUMN.index(k)
        for step in steps:
            if k * step > 0 or (abs(k) == 3 and q // 2 != (step + 1) // 2):
                continue
            to = k - step
            j = COLUMN.index(4 if abs(to) == 4 else to)
            copy(zpart(i, q), zpart(j, q), zsem.at[j, q], dev(0, 0, step, 0))

    def got_z(k, q):
        j = COLUMN.index(k)
        arrived(zpart(j, q), zsem.at[j, q])
        if k != 4:
            pass_z(k, q)

    def step_z(k, n):
        got_z(-k, (n + 2) % 4)
        got_z(k, n)

    def ready_c(*blocks):
        for i in blocks:
            for h in range(2):
                arrived(C.at[2 * i + 1, pl.ds(*HALVES[h])], ssem.at[i, h])
            for j in (2 * i, 2 * i + 1):
                low, high = keys_of(C[j, 0])
                low_key[j, 0:1, :] = low
                high_key[j, 0:1, :] = high

    def ready_r(*ks):
        for k in ks:
            u = COLUMN.index(k)
            _, high = keys_of(R[u, 0])
            row_key[u] = jnp.broadcast_to(high, (128, 128)).T

    def use(scores, blocks, ks):
        for a, k in enumerate(ks):
            u = COLUMN.index(k)
            key = row_key[u]
            side = acc_r[u]
            for b in range(2 * len(blocks)):
                j = 2 * blocks[b // 2] + b % 2
                part = scores[a * 128:(a + 1) * 128, b * 128:(b + 1) * 128]
                low = low_key[j, 0:1, :]
                high = high_key[j, 0:1, :]
                earlier = jnp.where((key >= low) & (key < high), part, jnp.float32(-1.0))
                acc_c[j] = jnp.maximum(acc_c[j], jnp.max(earlier.reshape(16, 8, 128), axis=0))
                side = jnp.maximum(side, jnp.where((key > high) & (key < low + 32768.0), part, jnp.float32(-1.0)))
            acc_r[u] = side

    def scores_of(blocks, ks, features=range(8)):
        rows = jnp.concatenate([rows_of(R, COLUMN.index(k), features) for k in ks], axis=0)
        columns = jnp.concatenate([columns_of(C, 2 * i + c, features) for i in blocks for c in range(2)], axis=1)
        return product(rows, columns)

    def compute(blocks, ks):
        use(scores_of(blocks, ks), blocks, ks)

    def answer_r(*ks):
        for k in ks:
            u = COLUMN.index(k)
            out_r[u] = jnp.max(acc_r[u].T.reshape(16, 8, 128), axis=0)
            if k:
                v = COLUMN.index(4 if k == 4 else -k)
                copy(out_r.at[u], res_r.at[v], rsem_r.at[v], dev(0, 0, k, 0))

    def answer_c(*blocks):
        for i in blocks:
            for c in range(2):
                j = 2 * i + c
                if j != 2 * OWN:
                    copy(acc_c.at[j], res_c.at[j], rsem_c.at[j], dev(PLANE[i][0], PLANE[i][1], 0, c))

    pl.semaphore_signal(corner_sem, inc=1, device_id=dev(-1, 0, 0, 0), device_id_type=MESH)

    for q in range(4):
        pass_z(0, (q + 2) % 4, (1,))
        pass_z(0, q, (-1,))
    for k in range(8):
        C[2 * OWN, 1 + k * 8:9 + k * 8] = unit[:, k * 128:(k + 1) * 128].T.astype(jnp.bfloat16).reshape(8, 16, 128)
    for q in range(4):
        for step, _ in ONWARD[(0, 0)]:
            pass_c((0, 0), step, q)
    share(OWN, 0)
    share(OWN, 1)
    acc_r[...] = jnp.full(acc_r.shape, -1.0, jnp.float32)
    acc_c[...] = jnp.full(acc_c.shape, -1.0, jnp.float32)
    pl.semaphore_wait(corner_sem, 1)
    for q in (2, 3, 0, 1):
        pass_c((0, 0), (1, 1), q)

    step_z(1, 0)
    got_c((1, 0), 0)
    got_c((0, 1), 0)
    step_z(1, 1)
    got_c((1, 0), 1)
    got_c((0, 1), 1)
    got_c((3, 3), 2)
    step_z(1, 2)
    got_c((1, 0), 2)
    got_c((0, 1), 2)
    got_c((3, 3), 3)
    step_z(1, 3)
    got_c((1, 0), 3)
    got_c((0, 1), 3)
    got_c((3, 3), 0)
    ready_r(0, 1, -1)
    ready_c(OWN)
    step_z(2, 0)
    got_c((2, 0), 0)
    got_c((0, 2), 0)
    got_c((3, 3), 1)
    ready_c(0, 1)
    compute((6, 0, 1), (0, 1, -1))
    step_z(2, 1)
    got_c((2, 0), 1)
    got_c((0, 2), 1)
    got_c((2, 3), 2)
    got_c((1, 3), 0)
    ready_c(2)
    step_z(2, 2)
    compute((2,), (0, 1, -1))
    got_c((2, 3), 3)
    got_c((1, 3), 1)
    got_c((2, 0), 2)
    got_c((0, 2), 2)
    got_c((3, 2), 2)
    got_c((2, 3), 0)
    step_z(2, 3)
    got_c((2, 0), 3)
    got_c((0, 2), 3)
    ready_r(2, -2)
    compute((6, 0, 1, 2), (2, -2))
    got_c((3, 2), 3)
    got_c((2, 3), 1)
    step_z(3, 0)
    ready_c(7, 8)
    compute((7, 8), (0, 1, 2))
    got_c((3, 2), 0)
    got_c((1, 3), 2)
    step_z(3, 1)
    ready_c(3)
    compute((3,), (0, 1, -1, 2, -2))
    got_c((3, 2), 1)
    got_c((1, 3), 3)
    step_z(3, 2)
    got_c((2, 2), 2, 0)
    ready_c(4, 5)
    step_z(3, 3)
    compute((4, 5), (0, 1, -1, 2, -2))
    got_c((2, 2), 3, 1)
    ready_r(3, -3)
    compute((0, 1, 2, 3, 4, 5), (3, -3))
    answer_r(-1, -2, -3)
    compute((6, 7, 8), (3,))
    got_z(4, 2)
    got_z(4, 0)
    ready_r(4)
    ready_c(9)
    compute((9,), (0, 1, 2, 3))
    every = tuple(range(10))
    half[...] = scores_of(every, (4,), EARLY)
    got_z(4, 3)
    got_z(4, 1)
    use(half[...] + scores_of(every, (4,), LATE), every, (4,))
    answer_c(9)
    answer_r(4)
    answer_c(3, 5, 4, 7, 8, 2, 0, 1, 6)
    answer_r(3, 2, 1, 0)

    for d in sends:
        d.wait_send()
    best = jnp.maximum(out_r[0], acc_c[2 * OWN])
    for u in range(1, 8):
        arrived(res_r.at[u], rsem_r.at[u])
        best = jnp.maximum(best, res_r[u])
    for j in range(20):
        if j != 2 * OWN:
            arrived(res_c.at[j], rsem_c.at[j])
            best = jnp.maximum(best, res_c[j])
    out_ref[...] = jnp.max(best, axis=0, keepdims=True)


def shards(embeddings, cluster_ids, row_order):
    out = pl.pallas_call(
        kernel,
        out_shape=jax.ShapeDtypeStruct((1, 128), jnp.float32),
        in_specs=[pl.BlockSpec(memory_space=pltpu.HBM)] * 3,
        out_specs=pl.BlockSpec(memory_space=pltpu.VMEM),
        scratch_shapes=[
            pltpu.VMEM((128, 1024), jnp.bfloat16),
            pltpu.VMEM((1, 128), jnp.int32),
            pltpu.VMEM((1, 128), jnp.int32),
            pltpu.SemaphoreType.DMA((3,)),
            pltpu.VMEM((20, CHUNKS, 16, 128), jnp.bfloat16),
            pltpu.VMEM((8, CHUNKS, 16, 128), jnp.bfloat16),
            pltpu.VMEM((8, 128, 128), jnp.float32),
            pltpu.VMEM((20, 8, 128), jnp.float32),
            pltpu.VMEM((20, 8, 128), jnp.float32),
            pltpu.VMEM((128, 2560), jnp.float32),
            pltpu.VMEM((8, 128, 128), jnp.float32),
            pltpu.VMEM((20, 8, 128), jnp.float32),
            pltpu.VMEM((8, 8, 128), jnp.float32),
            pltpu.VMEM((8, 8, 128), jnp.float32),
            pltpu.VMEM((20, 8, 128), jnp.float32),
            pltpu.SemaphoreType.DMA((128,)),
            pltpu.SemaphoreType.DMA((10, 4)),
            pltpu.SemaphoreType.DMA((10, 2)),
            pltpu.SemaphoreType.DMA((8, 4)),
            pltpu.SemaphoreType.DMA((8,)),
            pltpu.SemaphoreType.DMA((20,)),
            pltpu.SemaphoreType.REGULAR,
        ],
        compiler_params=pltpu.CompilerParams(collective_id=0, has_side_effects=True, vmem_limit_bytes=64 << 20),
        name="nearest_earlier",
    )(embeddings, cluster_ids.reshape(1, 128), row_order.reshape(1, 128))
    return out.reshape(128)


def solution(mesh):
    in_specs = (P(("grp", "blk"), None), P(("grp", "blk")), P(("grp", "blk")))
    return jax.shard_map(shards, mesh=mesh, in_specs=in_specs, out_specs=P(("grp", "blk")), check_vma=False)
```

```python
import jax
import jax.numpy as jnp
from jax import lax
from jax.experimental import pallas as pl
from jax.experimental.pallas import tpu as pltpu
from jax.sharding import PartitionSpec as P

MESH = pl.DeviceIdType.MESH
NX, NY, NZ = 4, 4, 8
CHUNKS = 65
HALVES = ((0, 33), (33, 32))
QUARTERS = ((0, 17), (17, 16), (33, 16), (49, 16))
EARLY, LATE = (0, 1, 4, 5), (2, 3, 6, 7)
PLANE = ((1, 0), (0, 1), (3, 3), (2, 3), (1, 3), (1, 2), (0, 0), (0, 2), (2, 0), (2, 2))
OWN = PLANE.index((0, 0))
COLUMN = (0, 1, -1, 2, -2, 3, -3, 4)
ONWARD = {
    (0, 0): (((-1, 0), (0, 1, 2, 3)), ((0, -1), (2, 3, 0, 1))),
    (1, 0): (((-1, 0), (0, 1)), ((0, 1), (0, 1))),
    (0, 1): (((0, -1), (0, 1, 2, 3)),),
    (0, 2): (((-1, 0), (0, 1, 2, 3)),),
    (3, 3): (((1, 0), (0, 1, 2, 3)),),
    (2, 3): (((1, 0), (2, 3)), ((0, -1), (2, 3)), ((0, 1), (0, 1, 2, 3))),
}


def rows_of(R, u, features=range(8)):
    return jnp.concatenate([R[u, 1 + k * 8:9 + k * 8].reshape(128, 128) for k in features], axis=1)


def columns_of(C, j, features=range(8)):
    return jnp.concatenate([C[j, 1 + k * 8:9 + k * 8].reshape(128, 128) for k in features], axis=0)


def product(rows, columns):
    return jnp.dot(rows, columns, preferred_element_type=jnp.float32)


def keys_of(tag):
    tag = tag.astype(jnp.float32)
    low = tag[0:1] * 32768.0
    return low, low + tag[1:2] * 256.0 + tag[2:3]


def kernel(emb_hbm, cid_hbm, ord_hbm, out_ref, emb_ref, cid_ref, ord_ref, in_sems, C, R, row_low, row_key, low_key, high_key, half, acc_r, acc_c, out_r, res_r, res_c, send_sems, csem, ssem, zsem, rsem_r, rsem_c, corner_sem):
    loads = [
        pltpu.make_async_copy(src, dst, in_sems.at[i])
        for i, (src, dst) in enumerate(((emb_hbm, emb_ref), (cid_hbm, cid_ref), (ord_hbm, ord_ref)))
    ]
    for load in loads:
        load.start()
    x = lax.axis_index("grp")
    blk = lax.axis_index("blk")
    core = lax.rem(blk, 2)
    y = lax.rem(lax.div(blk, 2), NY)
    z = lax.div(blk, 2 * NY)

    def dev(dx, dy, dz, dc):
        other = lax.rem(core + dc, 2)
        return (lax.rem(x + dx % NX, NX), (lax.rem(z + dz % NZ, NZ) * NY + lax.rem(y + dy % NY, NY)) * 2 + other)

    sib = dev(0, 0, 0, 1)

    barrier = pltpu.get_barrier_semaphore()
    near = [dev(1, 0, 0, 0), dev(-1, 0, 0, 0), dev(0, 1, 0, 0), dev(0, -1, 0, 0), dev(0, 0, 1, 0), dev(0, 0, -1, 0), sib]
    for target in near:
        pl.semaphore_signal(barrier, inc=1, device_id=target, device_id_type=MESH)

    for load in loads:
        load.wait()
    values = emb_ref[...].astype(jnp.float32)
    total = jnp.sum(values * values, axis=1, keepdims=True)
    unit = values * lax.rsqrt(total + 1e-06)
    for k in range(8):
        R[0, 1 + k * 8:9 + k * 8] = unit[:, k * 128:(k + 1) * 128].astype(jnp.bfloat16).reshape(8, 16, 128)
    row = lax.broadcasted_iota(jnp.int32, (16, 128), 0)
    order = ord_ref[...]
    tag = jnp.where(row == 0, cid_ref[...], jnp.where(row == 1, lax.shift_right_logical(order, 8), jnp.where(row == 2, order & 255, 0)))
    tag = tag.astype(jnp.float32).astype(jnp.bfloat16)
    C[2 * OWN, 0] = tag
    R[0, 0] = tag
    pl.semaphore_wait(barrier, len(near))

    sends = []

    def copy(src, dst, sem, target):
        d = pltpu.make_async_remote_copy(
            src_ref=src, dst_ref=dst, send_sem=send_sems.at[len(sends)], recv_sem=sem, device_id=target, device_id_type=MESH
        )
        d.start()
        sends.append(d)

    def arrived(dst, sem):
        pltpu.make_async_remote_copy(
            src_ref=dst, dst_ref=dst, send_sem=send_sems.at[0], recv_sem=sem, device_id=sib, device_id_type=MESH
        ).wait_recv()

    def cpart(i, q):
        return C.at[2 * i, pl.ds(*QUARTERS[q])]

    def zpart(u, q):
        return R.at[u, pl.ds(*QUARTERS[q])]

    def pass_c(d, step, q):
        i = PLANE.index(d)
        j = PLANE.index(((d[0] - step[0]) % NX, (d[1] - step[1]) % NY))
        copy(cpart(i, q), cpart(j, q), csem.at[j, q], dev(step[0], step[1], 0, 0))

    def share(i, h):
        copy(C.at[2 * i, pl.ds(*HALVES[h])], C.at[2 * i + 1, pl.ds(*HALVES[h])], ssem.at[i, h], sib)

    def got_c(d, *quarters):
        i = PLANE.index(d)
        for q in quarters:
            arrived(cpart(i, q), csem.at[i, q])
            for step, some in ONWARD.get(d, ()):
                if q in some:
                    pass_c(d, step, q)
            if q % 2:
                share(i, q // 2)

    def pass_z(k, q, steps=(1, -1)):
        i = COLUMN.index(k)
        for step in steps:
            if k * step > 0 or (abs(k) == 3 and q // 2 != (step + 1) // 2):
                continue
            to = k - step
            j = COLUMN.index(4 if abs(to) == 4 else to)
            copy(zpart(i, q), zpart(j, q), zsem.at[j, q], dev(0, 0, step, 0))

    def got_z(k, q):
        j = COLUMN.index(k)
        arrived(zpart(j, q), zsem.at[j, q])
        if k != 4:
            pass_z(k, q)

    def step_z(k, n):
        got_z(-k, (n + 2) % 4)
        got_z(k, n)

    def ready_c(*blocks):
        for i in blocks:
            for h in range(2):
                arrived(C.at[2 * i + 1, pl.ds(*HALVES[h])], ssem.at[i, h])
            for j in (2 * i, 2 * i + 1):
                low, high = keys_of(C[j, 0])
                low_key[j, 0:1, :] = low
                high_key[j, 0:1, :] = high

    def ready_r(*ks):
        for k in ks:
            u = COLUMN.index(k)
            low, high = keys_of(R[u, 0])
            row_low[u] = jnp.broadcast_to(low, (128, 128)).T
            row_key[u] = jnp.broadcast_to(high, (128, 128)).T

    def split(part, u, j):
        same = jnp.where(row_low[u] == low_key[j, 0:1, :], part, jnp.float32(-1.0))
        high = high_key[j, 0:1, :]
        before = row_key[u] < high
        if (u, j) == (0, 2 * OWN):
            return jnp.where(row_key[u] > high, same, jnp.float32(-1.0)), jnp.where(before, same, jnp.float32(-1.0))
        return jnp.where(before, jnp.float32(-1.0), same), jnp.where(before, same, jnp.float32(-1.0))

    def use(scores, blocks, ks):
        for a, k in enumerate(ks):
            u = COLUMN.index(k)
            side = acc_r[u]
            for b in range(2 * len(blocks)):
                j = 2 * blocks[b // 2] + b % 2
                later, earlier = split(scores[a * 128:(a + 1) * 128, b * 128:(b + 1) * 128], u, j)
                acc_c[j] = jnp.maximum(acc_c[j], jnp.max(earlier.reshape(16, 8, 128), axis=0))
                side = jnp.maximum(side, later)
            acc_r[u] = side

    def scores_of(blocks, ks, features=range(8)):
        rows = jnp.concatenate([rows_of(R, COLUMN.index(k), features) for k in ks], axis=0)
        columns = jnp.concatenate([columns_of(C, 2 * i + c, features) for i in blocks for c in range(2)], axis=1)
        return product(rows, columns)

    def compute(blocks, ks):
        use(scores_of(blocks, ks), blocks, ks)

    def answer_r(*ks):
        for k in ks:
            u = COLUMN.index(k)
            out_r[u] = jnp.max(acc_r[u].T.reshape(16, 8, 128), axis=0)
            if k:
                v = COLUMN.index(4 if k == 4 else -k)
                copy(out_r.at[u], res_r.at[v], rsem_r.at[v], dev(0, 0, k, 0))

    def answer_c(*blocks):
        for i in blocks:
            for c in range(2):
                j = 2 * i + c
                if j != 2 * OWN:
                    copy(acc_c.at[j], res_c.at[j], rsem_c.at[j], dev(PLANE[i][0], PLANE[i][1], 0, c))

    pl.semaphore_signal(corner_sem, inc=1, device_id=dev(-1, 0, 0, 0), device_id_type=MESH)

    for q in range(4):
        pass_z(0, (q + 2) % 4, (1,))
        pass_z(0, q, (-1,))
    for k in range(8):
        C[2 * OWN, 1 + k * 8:9 + k * 8] = unit[:, k * 128:(k + 1) * 128].T.astype(jnp.bfloat16).reshape(8, 16, 128)
    for q in range(4):
        for step, order in ONWARD[(0, 0)]:
            pass_c((0, 0), step, order[q])
    share(OWN, 0)
    share(OWN, 1)
    acc_r[...] = jnp.full(acc_r.shape, -1.0, jnp.float32)
    acc_c[...] = jnp.full(acc_c.shape, -1.0, jnp.float32)
    pl.semaphore_wait(corner_sem, 1)
    for q in (2, 3, 0, 1):
        pass_c((0, 0), (1, 1), q)

    step_z(1, 0)
    got_c((1, 0), 0)
    got_c((0, 1), 2)
    step_z(1, 1)
    got_c((1, 0), 1)
    got_c((0, 1), 3)
    got_c((3, 3), 2)
    step_z(1, 2)
    got_c((0, 1), 0)
    got_c((1, 0), 2)
    got_c((3, 3), 3)
    step_z(1, 3)
    got_c((0, 1), 1)
    got_c((1, 0), 3)
    got_c((3, 3), 0)
    ready_r(0, 1, -1)
    ready_c(OWN)
    step_z(2, 0)
    got_c((0, 2), 2)
    got_c((3, 3), 1)
    ready_c(0, 1)
    compute((6, 0, 1), (0, 1, -1))
    step_z(2, 1)
    got_c((2, 3), 2)
    got_c((0, 2), 3)
    ready_c(2)
    step_z(2, 2)
    compute((2,), (0, 1, -1))
    got_c((2, 3), 3)
    got_c((0, 2), 0)
    got_c((2, 3), 0)
    step_z(2, 3)
    got_c((0, 2), 1)
    ready_r(2, -2)
    compute((6, 0, 1, 2), (2, -2))
    got_c((2, 3), 1)
    got_c((1, 3), 0, 1)
    step_z(3, 0)
    ready_c(7)
    compute((7,), (0, 1, 2))
    got_c((2, 0), 0, 1, 2)
    got_c((1, 2), 2)
    step_z(3, 1)
    ready_c(3)
    compute((3,), (0, 1, -1, 2, -2))
    got_c((2, 0), 3)
    got_c((1, 2), 3)
    got_c((1, 3), 2)
    step_z(3, 2)
    ready_c(8)
    compute((8,), (0, 1, 2))
    got_c((1, 3), 3)
    got_c((1, 2), 0, 1)
    step_z(3, 3)
    got_c((2, 2), 2, 3)
    ready_r(3, -3)
    compute((0, 1, 2, 3), (3, -3))
    got_c((2, 2), 0, 1)
    ready_c(4, 5)
    compute((4, 5), (0, 1, -1, 2, -2, 3, -3))
    answer_r(-1, -2, -3)
    ready_c(9)
    compute((6, 7, 8, 9), (3,))
    compute((9,), (0, 1, 2))
    got_z(4, 2)
    got_z(4, 0)
    ready_r(4)
    every = tuple(range(10))
    half[...] = scores_of(every, (4,), EARLY)
    got_z(4, 3)
    got_z(4, 1)
    half[...] += scores_of(every, (4,), LATE)
    side = acc_r[7]
    for j in range(20):
        side = jnp.maximum(side, split(half[:, j * 128:(j + 1) * 128], 7, j)[0])
    acc_r[7] = side
    answer_r(4)
    for i in (9, 3, 5, 4, 7, 8, 2, 0, 1, 6):
        for j in (2 * i, 2 * i + 1):
            earlier = split(half[:, j * 128:(j + 1) * 128], 7, j)[1]
            acc_c[j] = jnp.maximum(acc_c[j], jnp.max(earlier.reshape(16, 8, 128), axis=0))
        answer_c(i)
    answer_r(3, 2, 1, 0)

    for d in sends:
        d.wait_send()
    best = jnp.maximum(out_r[0], acc_c[2 * OWN])
    for u in range(1, 8):
        arrived(res_r.at[u], rsem_r.at[u])
        best = jnp.maximum(best, res_r[u])
    for j in range(20):
        if j != 2 * OWN:
            arrived(res_c.at[j], rsem_c.at[j])
            best = jnp.maximum(best, res_c[j])
    out_ref[...] = jnp.max(best, axis=0, keepdims=True)


def shards(embeddings, cluster_ids, row_order):
    out = pl.pallas_call(
        kernel,
        out_shape=jax.ShapeDtypeStruct((1, 128), jnp.float32),
        in_specs=[pl.BlockSpec(memory_space=pltpu.HBM)] * 3,
        out_specs=pl.BlockSpec(memory_space=pltpu.VMEM),
        scratch_shapes=[
            pltpu.VMEM((128, 1024), jnp.bfloat16),
            pltpu.VMEM((1, 128), jnp.int32),
            pltpu.VMEM((1, 128), jnp.int32),
            pltpu.SemaphoreType.DMA((3,)),
            pltpu.VMEM((20, CHUNKS, 16, 128), jnp.bfloat16),
            pltpu.VMEM((8, CHUNKS, 16, 128), jnp.bfloat16),
            pltpu.VMEM((8, 128, 128), jnp.float32),
            pltpu.VMEM((8, 128, 128), jnp.float32),
            pltpu.VMEM((20, 8, 128), jnp.float32),
            pltpu.VMEM((20, 8, 128), jnp.float32),
            pltpu.VMEM((128, 2560), jnp.float32),
            pltpu.VMEM((8, 128, 128), jnp.float32),
            pltpu.VMEM((20, 8, 128), jnp.float32),
            pltpu.VMEM((8, 8, 128), jnp.float32),
            pltpu.VMEM((8, 8, 128), jnp.float32),
            pltpu.VMEM((20, 8, 128), jnp.float32),
            pltpu.SemaphoreType.DMA((128,)),
            pltpu.SemaphoreType.DMA((10, 4)),
            pltpu.SemaphoreType.DMA((10, 2)),
            pltpu.SemaphoreType.DMA((8, 4)),
            pltpu.SemaphoreType.DMA((8,)),
            pltpu.SemaphoreType.DMA((20,)),
            pltpu.SemaphoreType.REGULAR,
        ],
        compiler_params=pltpu.CompilerParams(collective_id=0, has_side_effects=True, vmem_limit_bytes=64 << 20),
        name="nearest_earlier",
    )(embeddings, cluster_ids.reshape(1, 128), row_order.reshape(1, 128))
    return out.reshape(128)


def solution(mesh):
    in_specs = (P(("grp", "blk"), None), P(("grp", "blk")), P(("grp", "blk")))
    return jax.shard_map(shards, mesh=mesh, in_specs=in_specs, out_specs=P(("grp", "blk")), check_vma=False)
```

```python
import jax
import jax.numpy as jnp
from jax import lax
from jax.experimental import pallas as pl
from jax.experimental.pallas import tpu as pltpu
from jax.sharding import PartitionSpec as P

MESH = pl.DeviceIdType.MESH
NX, NY, NZ = 4, 4, 8
CHUNKS = 65
HALVES = ((0, 33), (33, 32))
QUARTERS = ((0, 17), (17, 16), (33, 16), (49, 16))
EARLY, LATE = (0, 1, 4, 5), (2, 3, 6, 7)
PLANE = ((1, 0), (0, 1), (3, 3), (2, 3), (1, 3), (1, 2), (0, 0), (0, 2), (2, 0), (2, 2))
OWN = PLANE.index((0, 0))
COLUMN = (0, 1, -1, 2, -2, 3, -3, 4)
ONWARD = {
    (0, 0): (((-1, 0), (0, 1, 2, 3)), ((0, -1), (2, 3, 0, 1))),
    (1, 0): (((-1, 0), (0, 1)), ((0, 1), (0, 1))),
    (0, 1): (((0, -1), (0, 1, 2, 3)),),
    (0, 2): (((-1, 0), (0, 1, 2, 3)),),
    (3, 3): (((1, 0), (0, 1, 2, 3)),),
    (2, 3): (((1, 0), (2, 3)), ((0, -1), (2, 3)), ((0, 1), (0, 1, 2, 3))),
}


def rows_of(R, u, features=range(8)):
    return jnp.concatenate([R[u, 1 + k * 8:9 + k * 8].reshape(128, 128) for k in features], axis=1)


def columns_of(C, j, features=range(8)):
    return jnp.concatenate([C[j, 1 + k * 8:9 + k * 8].reshape(128, 128) for k in features], axis=0)


def product(rows, columns):
    return jnp.dot(rows, columns, preferred_element_type=jnp.float32)


def keys_of(tag):
    tag = tag.astype(jnp.float32)
    low = tag[0:1] * 32768.0
    return low, low + tag[1:2] * 256.0 + tag[2:3]


def kernel(emb_hbm, cid_ref, ord_ref, out_ref, emb_ref, in_sem, C, R, row_low, row_key, low_key, high_key, half, acc_r, acc_c, out_r, res_r, res_c, send_sems, csem, ssem, zsem, rsem_r, rsem_c, corner_sem):
    load = pltpu.make_async_copy(emb_hbm, emb_ref, in_sem)
    load.start()
    x = lax.axis_index("grp")
    blk = lax.axis_index("blk")
    core = lax.rem(blk, 2)
    y = lax.rem(lax.div(blk, 2), NY)
    z = lax.div(blk, 2 * NY)

    def dev(dx, dy, dz, dc):
        other = lax.rem(core + dc, 2)
        return (lax.rem(x + dx % NX, NX), (lax.rem(z + dz % NZ, NZ) * NY + lax.rem(y + dy % NY, NY)) * 2 + other)

    sib = dev(0, 0, 0, 1)

    barrier = pltpu.get_barrier_semaphore()
    near = [dev(1, 0, 0, 0), dev(-1, 0, 0, 0), dev(0, 1, 0, 0), dev(0, -1, 0, 0), dev(0, 0, 1, 0), dev(0, 0, -1, 0), sib]
    for target in near:
        pl.semaphore_signal(barrier, inc=1, device_id=target, device_id_type=MESH)

    load.wait()
    values = emb_ref[...].astype(jnp.float32)
    total = jnp.sum(values * values, axis=1, keepdims=True)
    unit = values * lax.rsqrt(total + 1e-06)
    for k in range(8):
        R[0, 1 + k * 8:9 + k * 8] = unit[:, k * 128:(k + 1) * 128].astype(jnp.bfloat16).reshape(8, 16, 128)
    row = lax.broadcasted_iota(jnp.int32, (16, 128), 0)
    order = ord_ref[...]
    tag = jnp.where(row == 0, cid_ref[...], jnp.where(row == 1, lax.shift_right_logical(order, 8), jnp.where(row == 2, order & 255, 0)))
    tag = tag.astype(jnp.float32).astype(jnp.bfloat16)
    C[2 * OWN, 0] = tag
    R[0, 0] = tag
    pl.semaphore_wait(barrier, len(near))

    sends = []

    def copy(src, dst, sem, target):
        d = pltpu.make_async_remote_copy(
            src_ref=src, dst_ref=dst, send_sem=send_sems.at[len(sends)], recv_sem=sem, device_id=target, device_id_type=MESH
        )
        d.start()
        sends.append(d)

    def arrived(dst, sem):
        pltpu.make_async_remote_copy(
            src_ref=dst, dst_ref=dst, send_sem=send_sems.at[0], recv_sem=sem, device_id=sib, device_id_type=MESH
        ).wait_recv()

    def cpart(i, q):
        return C.at[2 * i, pl.ds(*QUARTERS[q])]

    def zpart(u, q):
        return R.at[u, pl.ds(*QUARTERS[q])]

    def pass_c(d, step, q):
        i = PLANE.index(d)
        j = PLANE.index(((d[0] - step[0]) % NX, (d[1] - step[1]) % NY))
        copy(cpart(i, q), cpart(j, q), csem.at[j, q], dev(step[0], step[1], 0, 0))

    def share(i, h):
        copy(C.at[2 * i, pl.ds(*HALVES[h])], C.at[2 * i + 1, pl.ds(*HALVES[h])], ssem.at[i, h], sib)

    def got_c(d, *quarters):
        i = PLANE.index(d)
        for q in quarters:
            arrived(cpart(i, q), csem.at[i, q])
            for step, some in ONWARD.get(d, ()):
                if q in some:
                    pass_c(d, step, q)
            if q % 2:
                share(i, q // 2)

    def pass_z(k, q, steps=(1, -1)):
        i = COLUMN.index(k)
        for step in steps:
            if k * step > 0 or (abs(k) == 3 and q // 2 != (step + 1) // 2):
                continue
            to = k - step
            j = COLUMN.index(4 if abs(to) == 4 else to)
            copy(zpart(i, q), zpart(j, q), zsem.at[j, q], dev(0, 0, step, 0))

    def got_z(k, q):
        j = COLUMN.index(k)
        arrived(zpart(j, q), zsem.at[j, q])
        if k != 4:
            pass_z(k, q)

    def step_z(k, n):
        got_z(-k, (n + 2) % 4)
        got_z(k, n)

    def ready_c(*blocks):
        for i in blocks:
            for h in range(2):
                arrived(C.at[2 * i + 1, pl.ds(*HALVES[h])], ssem.at[i, h])
            for j in (2 * i, 2 * i + 1):
                low, high = keys_of(C[j, 0])
                low_key[j, 0:1, :] = low
                high_key[j, 0:1, :] = high

    def ready_r(*ks):
        for k in ks:
            u = COLUMN.index(k)
            low, high = keys_of(R[u, 0])
            row_low[u] = jnp.broadcast_to(low, (128, 128)).T
            row_key[u] = jnp.broadcast_to(high, (128, 128)).T

    def split(part, u, j):
        same = jnp.where(row_low[u] == low_key[j, 0:1, :], part, jnp.float32(-1.0))
        high = high_key[j, 0:1, :]
        before = row_key[u] < high
        if (u, j) == (0, 2 * OWN):
            return jnp.where(row_key[u] > high, same, jnp.float32(-1.0)), jnp.where(before, same, jnp.float32(-1.0))
        return jnp.where(before, jnp.float32(-1.0), same), jnp.where(before, same, jnp.float32(-1.0))

    def use(scores, blocks, ks):
        for a, k in enumerate(ks):
            u = COLUMN.index(k)
            side = acc_r[u]
            for b in range(2 * len(blocks)):
                j = 2 * blocks[b // 2] + b % 2
                later, earlier = split(scores[a * 128:(a + 1) * 128, b * 128:(b + 1) * 128], u, j)
                acc_c[j] = jnp.maximum(acc_c[j], jnp.max(earlier.reshape(16, 8, 128), axis=0))
                side = jnp.maximum(side, later)
            acc_r[u] = side

    def scores_of(blocks, ks, features=range(8)):
        rows = jnp.concatenate([rows_of(R, COLUMN.index(k), features) for k in ks], axis=0)
        columns = jnp.concatenate([columns_of(C, 2 * i + c, features) for i in blocks for c in range(2)], axis=1)
        return product(rows, columns)

    def compute(blocks, ks):
        use(scores_of(blocks, ks), blocks, ks)

    def answer_r(*ks):
        for k in ks:
            u = COLUMN.index(k)
            out_r[u] = jnp.max(acc_r[u].T.reshape(16, 8, 128), axis=0)
            if k:
                v = COLUMN.index(4 if k == 4 else -k)
                copy(out_r.at[u], res_r.at[v], rsem_r.at[v], dev(0, 0, k, 0))

    def answer_c(*blocks):
        for i in blocks:
            for c in range(2):
                j = 2 * i + c
                if j != 2 * OWN:
                    copy(acc_c.at[j], res_c.at[j], rsem_c.at[j], dev(PLANE[i][0], PLANE[i][1], 0, c))

    pl.semaphore_signal(corner_sem, inc=1, device_id=dev(-1, 0, 0, 0), device_id_type=MESH)

    for q in range(4):
        pass_z(0, (q + 2) % 4, (1,))
        pass_z(0, q, (-1,))
    for k in range(8):
        C[2 * OWN, 1 + k * 8:9 + k * 8] = unit[:, k * 128:(k + 1) * 128].T.astype(jnp.bfloat16).reshape(8, 16, 128)
    for q in range(4):
        for step, order in ONWARD[(0, 0)]:
            pass_c((0, 0), step, order[q])
    share(OWN, 0)
    share(OWN, 1)
    acc_r[...] = jnp.full(acc_r.shape, -1.0, jnp.float32)
    acc_c[...] = jnp.full(acc_c.shape, -1.0, jnp.float32)
    pl.semaphore_wait(corner_sem, 1)
    for q in (2, 3, 0, 1):
        pass_c((0, 0), (1, 1), q)

    step_z(1, 0)
    got_c((1, 0), 0)
    got_c((0, 1), 2)
    step_z(1, 1)
    got_c((1, 0), 1)
    got_c((0, 1), 3)
    got_c((3, 3), 2)
    step_z(1, 2)
    got_c((0, 1), 0)
    got_c((1, 0), 2)
    got_c((3, 3), 3)
    step_z(1, 3)
    got_c((0, 1), 1)
    got_c((1, 0), 3)
    got_c((3, 3), 0)
    ready_r(0, 1, -1)
    ready_c(OWN)
    step_z(2, 0)
    got_c((0, 2), 2)
    got_c((3, 3), 1)
    ready_c(0, 1)
    compute((6, 0, 1), (0, 1, -1))
    step_z(2, 1)
    got_c((2, 3), 2)
    got_c((0, 2), 3)
    ready_c(2)
    step_z(2, 2)
    compute((2,), (0, 1, -1))
    got_c((2, 3), 3)
    got_c((0, 2), 0)
    got_c((2, 3), 0)
    step_z(2, 3)
    got_c((0, 2), 1)
    ready_r(2, -2)
    compute((6, 0, 1, 2), (2, -2))
    got_c((2, 3), 1)
    got_c((1, 3), 0, 1)
    step_z(3, 0)
    ready_c(7)
    compute((7,), (0, 1, 2))
    got_c((2, 0), 0, 1, 2)
    got_c((1, 2), 2)
    step_z(3, 1)
    ready_c(3)
    compute((3,), (0, 1, -1, 2, -2))
    got_c((2, 0), 3)
    got_c((1, 2), 3)
    got_c((1, 3), 2)
    step_z(3, 2)
    ready_c(8)
    compute((8,), (0, 1, 2))
    got_c((1, 3), 3)
    got_c((1, 2), 0, 1)
    step_z(3, 3)
    got_c((2, 2), 2, 3)
    ready_r(3, -3)
    compute((0, 1, 2, 3), (3, -3))
    got_c((2, 2), 0, 1)
    ready_c(4, 5)
    compute((4, 5), (0, 1, -1, 2, -2, 3, -3))
    answer_r(-1, -2, -3)
    compute((6, 7, 8), (3,))
    got_z(4, 2)
    got_z(4, 0)
    ready_r(4)
    ready_c(9)
    compute((9,), (0, 1, 2, 3))
    every = tuple(range(10))
    half[...] = scores_of(every, (4,), EARLY)
    got_z(4, 3)
    got_z(4, 1)
    half[...] += scores_of(every, (4,), LATE)
    side = acc_r[7]
    for j in range(20):
        side = jnp.maximum(side, split(half[:, j * 128:(j + 1) * 128], 7, j)[0])
    acc_r[7] = side
    answer_r(4, 3)
    for i in (9, 3, 5, 4, 7, 8, 2, 0, 1, 6):
        for j in (2 * i, 2 * i + 1):
            earlier = split(half[:, j * 128:(j + 1) * 128], 7, j)[1]
            acc_c[j] = jnp.maximum(acc_c[j], jnp.max(earlier.reshape(16, 8, 128), axis=0))
        answer_c(i)
    answer_r(2, 1, 0)

    for d in sends:
        d.wait_send()
    best = jnp.maximum(out_r[0], acc_c[2 * OWN])
    for u in range(1, 8):
        arrived(res_r.at[u], rsem_r.at[u])
        best = jnp.maximum(best, res_r[u])
    for j in range(20):
        if j != 2 * OWN:
            arrived(res_c.at[j], rsem_c.at[j])
            best = jnp.maximum(best, res_c[j])
    out_ref[...] = jnp.max(best, axis=0, keepdims=True)


def shards(embeddings, cluster_ids, row_order):
    out = pl.pallas_call(
        kernel,
        out_shape=jax.ShapeDtypeStruct((1, 128), jnp.float32),
        in_specs=[pl.BlockSpec(memory_space=pltpu.HBM)] + [pl.BlockSpec(memory_space=pltpu.VMEM)] * 2,
        out_specs=pl.BlockSpec(memory_space=pltpu.VMEM),
        scratch_shapes=[
            pltpu.VMEM((128, 1024), jnp.bfloat16),
            pltpu.SemaphoreType.DMA,
            pltpu.VMEM((20, CHUNKS, 16, 128), jnp.bfloat16),
            pltpu.VMEM((8, CHUNKS, 16, 128), jnp.bfloat16),
            pltpu.VMEM((8, 128, 128), jnp.float32),
            pltpu.VMEM((8, 128, 128), jnp.float32),
            pltpu.VMEM((20, 8, 128), jnp.float32),
            pltpu.VMEM((20, 8, 128), jnp.float32),
            pltpu.VMEM((128, 2560), jnp.float32),
            pltpu.VMEM((8, 128, 128), jnp.float32),
            pltpu.VMEM((20, 8, 128), jnp.float32),
            pltpu.VMEM((8, 8, 128), jnp.float32),
            pltpu.VMEM((8, 8, 128), jnp.float32),
            pltpu.VMEM((20, 8, 128), jnp.float32),
            pltpu.SemaphoreType.DMA((128,)),
            pltpu.SemaphoreType.DMA((10, 4)),
            pltpu.SemaphoreType.DMA((10, 2)),
            pltpu.SemaphoreType.DMA((8, 4)),
            pltpu.SemaphoreType.DMA((8,)),
            pltpu.SemaphoreType.DMA((20,)),
            pltpu.SemaphoreType.REGULAR,
        ],
        compiler_params=pltpu.CompilerParams(collective_id=0, has_side_effects=True, vmem_limit_bytes=56475648),
        name="nearest_earlier",
    )(embeddings, cluster_ids.reshape(1, 128), row_order.reshape(1, 128))
    return out.reshape(128)


def solution(mesh):
    in_specs = (P(("grp", "blk"), None), P(("grp", "blk")), P(("grp", "blk")))
    return jax.shard_map(shards, mesh=mesh, in_specs=in_specs, out_specs=P(("grp", "blk")), check_vma=False)
```

```python
import jax
import jax.numpy as jnp
from jax import lax
from jax.experimental import pallas as pl
from jax.experimental.pallas import tpu as pltpu
from jax.sharding import PartitionSpec as P

MESH = pl.DeviceIdType.MESH
NX, NY, NZ = 4, 4, 8
CHUNKS = 65
HALVES = ((0, 33), (33, 32))
QUARTERS = ((0, 17), (17, 16), (33, 16), (49, 16))
EARLY, LATE = (0, 1, 4, 5), (2, 3, 6, 7)
PLANE = ((1, 0), (0, 1), (3, 3), (2, 3), (1, 3), (1, 2), (0, 0), (0, 2), (2, 0), (2, 2))
OWN = PLANE.index((0, 0))
COLUMN = (0, 1, -1, 2, -2, 3, -3, 4)
ONWARD = {
    (0, 0): (((-1, 0), (0, 1, 2, 3)), ((0, -1), (2, 3, 0, 1))),
    (1, 0): (((-1, 0), (0, 1)), ((0, 1), (0, 1))),
    (0, 1): (((0, -1), (0, 1, 2, 3)),),
    (0, 2): (((-1, 0), (0, 1, 2, 3)),),
    (3, 3): (((1, 0), (0, 1, 2, 3)),),
    (2, 3): (((1, 0), (2, 3)), ((0, -1), (2, 3)), ((0, 1), (0, 1, 2, 3))),
}


def rows_of(R, u, features=range(8)):
    return jnp.concatenate([R[u, 1 + k * 8:9 + k * 8].reshape(128, 128) for k in features], axis=1)


def columns_of(C, j, features=range(8)):
    return jnp.concatenate([C[j, 1 + k * 8:9 + k * 8].reshape(128, 128) for k in features], axis=0)


def product(rows, columns):
    return jnp.dot(rows, columns, preferred_element_type=jnp.float32)


def keys_of(tag):
    tag = tag.astype(jnp.float32)
    low = tag[0:1] * 32768.0
    return low, low + tag[1:2] * 256.0 + tag[2:3]


def kernel(emb_hbm, cid_ref, ord_ref, out_ref, emb_ref, in_sem, C, R, row_low, row_key, low_key, high_key, half, acc_r, acc_c, out_r, res_r, res_c, send_sems, csem, ssem, zsem, rsem_r, rsem_c, corner_sem):
    load = pltpu.make_async_copy(emb_hbm, emb_ref, in_sem)
    load.start()
    x = lax.axis_index("grp")
    blk = lax.axis_index("blk")
    core = lax.rem(blk, 2)
    y = lax.rem(lax.div(blk, 2), NY)
    z = lax.div(blk, 2 * NY)

    def dev(dx, dy, dz, dc):
        other = lax.rem(core + dc, 2)
        return (lax.rem(x + dx % NX, NX), (lax.rem(z + dz % NZ, NZ) * NY + lax.rem(y + dy % NY, NY)) * 2 + other)

    sib = dev(0, 0, 0, 1)

    barrier = pltpu.get_barrier_semaphore()
    near = [dev(1, 0, 0, 0), dev(-1, 0, 0, 0), dev(0, 1, 0, 0), dev(0, -1, 0, 0), dev(0, 0, 1, 0), dev(0, 0, -1, 0), sib]
    for target in near:
        pl.semaphore_signal(barrier, inc=1, device_id=target, device_id_type=MESH)

    load.wait()
    values = emb_ref[...].astype(jnp.float32)
    total = jnp.sum(values * values, axis=1, keepdims=True)
    unit = values * lax.rsqrt(total + 1e-06)
    for k in range(8):
        R[0, 1 + k * 8:9 + k * 8] = unit[:, k * 128:(k + 1) * 128].astype(jnp.bfloat16).reshape(8, 16, 128)
    row = lax.broadcasted_iota(jnp.int32, (16, 128), 0)
    order = ord_ref[...]
    tag = jnp.where(row == 0, cid_ref[...], jnp.where(row == 1, lax.shift_right_logical(order, 8), jnp.where(row == 2, order & 255, 0)))
    tag = tag.astype(jnp.float32).astype(jnp.bfloat16)
    C[2 * OWN, 0] = tag
    R[0, 0] = tag
    pl.semaphore_wait(barrier, len(near))

    sends = []

    def copy(src, dst, sem, target):
        d = pltpu.make_async_remote_copy(
            src_ref=src, dst_ref=dst, send_sem=send_sems.at[len(sends)], recv_sem=sem, device_id=target, device_id_type=MESH
        )
        d.start()
        sends.append(d)

    def arrived(dst, sem):
        pltpu.make_async_remote_copy(
            src_ref=dst, dst_ref=dst, send_sem=send_sems.at[0], recv_sem=sem, device_id=sib, device_id_type=MESH
        ).wait_recv()

    def cpart(i, q):
        return C.at[2 * i, pl.ds(*QUARTERS[q])]

    def zpart(u, q):
        return R.at[u, pl.ds(*QUARTERS[q])]

    def pass_c(d, step, q):
        i = PLANE.index(d)
        j = PLANE.index(((d[0] - step[0]) % NX, (d[1] - step[1]) % NY))
        copy(cpart(i, q), cpart(j, q), csem.at[j, q], dev(step[0], step[1], 0, 0))

    def share(i, h):
        copy(C.at[2 * i, pl.ds(*HALVES[h])], C.at[2 * i + 1, pl.ds(*HALVES[h])], ssem.at[i, h], sib)

    def got_c(d, *quarters):
        i = PLANE.index(d)
        for q in quarters:
            arrived(cpart(i, q), csem.at[i, q])
            for step, some in ONWARD.get(d, ()):
                if q in some:
                    pass_c(d, step, q)
            if q % 2:
                share(i, q // 2)

    def pass_z(k, q, steps=(1, -1)):
        i = COLUMN.index(k)
        for step in steps:
            if k * step > 0 or (abs(k) == 3 and q // 2 != (step + 1) // 2):
                continue
            to = k - step
            j = COLUMN.index(4 if abs(to) == 4 else to)
            copy(zpart(i, q), zpart(j, q), zsem.at[j, q], dev(0, 0, step, 0))

    def got_z(k, q):
        j = COLUMN.index(k)
        arrived(zpart(j, q), zsem.at[j, q])
        if k != 4:
            pass_z(k, q)

    def step_z(k, n):
        got_z(-k, (n + 2) % 4)
        got_z(k, n)

    def ready_c(*blocks):
        for i in blocks:
            for h in range(2):
                arrived(C.at[2 * i + 1, pl.ds(*HALVES[h])], ssem.at[i, h])
            for j in (2 * i, 2 * i + 1):
                low, high = keys_of(C[j, 0])
                low_key[j, 0:1, :] = low
                high_key[j, 0:1, :] = high

    def ready_r(*ks):
        for k in ks:
            u = COLUMN.index(k)
            low, high = keys_of(R[u, 0])
            row_low[u] = jnp.broadcast_to(low, (128, 128)).T
            row_key[u] = jnp.broadcast_to(high, (128, 128)).T

    def split(part, u, j):
        same = jnp.where(row_low[u] == low_key[j, 0:1, :], part, jnp.float32(-1.0))
        high = high_key[j, 0:1, :]
        before = row_key[u] < high
        if (u, j) == (0, 2 * OWN):
            return jnp.where(row_key[u] > high, same, jnp.float32(-1.0)), jnp.where(before, same, jnp.float32(-1.0))
        return jnp.where(before, jnp.float32(-1.0), same), jnp.where(before, same, jnp.float32(-1.0))

    def use(scores, blocks, ks):
        for a, k in enumerate(ks):
            u = COLUMN.index(k)
            side = acc_r[u]
            for b in range(2 * len(blocks)):
                j = 2 * blocks[b // 2] + b % 2
                later, earlier = split(scores[a * 128:(a + 1) * 128, b * 128:(b + 1) * 128], u, j)
                acc_c[j] = jnp.maximum(acc_c[j], jnp.max(earlier.reshape(16, 8, 128), axis=0))
                side = jnp.maximum(side, later)
            acc_r[u] = side

    def scores_of(blocks, ks, features=range(8)):
        rows = jnp.concatenate([rows_of(R, COLUMN.index(k), features) for k in ks], axis=0)
        columns = jnp.concatenate([columns_of(C, 2 * i + c, features) for i in blocks for c in range(2)], axis=1)
        return product(rows, columns)

    def compute(blocks, ks):
        use(scores_of(blocks, ks), blocks, ks)

    def answer_r(*ks):
        for k in ks:
            u = COLUMN.index(k)
            out_r[u] = jnp.max(acc_r[u].T.reshape(16, 8, 128), axis=0)
            if k:
                v = COLUMN.index(4 if k == 4 else -k)
                copy(out_r.at[u], res_r.at[v], rsem_r.at[v], dev(0, 0, k, 0))

    def answer_c(*blocks):
        for i in blocks:
            for c in range(2):
                j = 2 * i + c
                if j != 2 * OWN:
                    copy(acc_c.at[j], res_c.at[j], rsem_c.at[j], dev(PLANE[i][0], PLANE[i][1], 0, c))

    pl.semaphore_signal(corner_sem, inc=1, device_id=dev(-1, 0, 0, 0), device_id_type=MESH)

    for q in range(4):
        pass_z(0, (q + 2) % 4, (1,))
        pass_z(0, q, (-1,))
    for k in range(8):
        C[2 * OWN, 1 + k * 8:9 + k * 8] = unit[:, k * 128:(k + 1) * 128].T.astype(jnp.bfloat16).reshape(8, 16, 128)
    for q in range(4):
        for step, order in ONWARD[(0, 0)]:
            pass_c((0, 0), step, order[q])
    share(OWN, 0)
    share(OWN, 1)
    acc_r[...] = jnp.full(acc_r.shape, -1.0, jnp.float32)
    acc_c[...] = jnp.full(acc_c.shape, -1.0, jnp.float32)
    pl.semaphore_wait(corner_sem, 1)
    for q in (2, 3, 0, 1):
        pass_c((0, 0), (1, 1), q)

    step_z(1, 0)
    got_c((1, 0), 0)
    got_c((0, 1), 2)
    step_z(1, 1)
    got_c((1, 0), 1)
    got_c((0, 1), 3)
    got_c((3, 3), 2)
    step_z(1, 2)
    got_c((0, 1), 0)
    got_c((1, 0), 2)
    got_c((3, 3), 3)
    step_z(1, 3)
    got_c((0, 1), 1)
    got_c((1, 0), 3)
    got_c((3, 3), 0)
    ready_r(0, 1, -1)
    ready_c(OWN)
    step_z(2, 0)
    got_c((0, 2), 2)
    got_c((3, 3), 1)
    ready_c(0, 1)
    compute((6, 0, 1), (0, 1, -1))
    step_z(2, 1)
    got_c((2, 3), 2)
    got_c((0, 2), 3)
    ready_c(2)
    step_z(2, 2)
    compute((2,), (0, 1, -1))
    got_c((2, 3), 3)
    got_c((0, 2), 0)
    got_c((2, 3), 0)
    step_z(2, 3)
    got_c((0, 2), 1)
    ready_r(2, -2)
    compute((6, 0, 1, 2), (2, -2))
    got_c((2, 3), 1)
    got_c((1, 3), 0, 1)
    step_z(3, 0)
    ready_c(7)
    compute((7,), (0, 1, 2))
    got_c((2, 0), 0, 1, 2)
    got_c((1, 2), 2)
    step_z(3, 1)
    ready_c(3)
    compute((3,), (0, 1, -1, 2, -2))
    got_c((2, 0), 3)
    got_c((1, 2), 3)
    got_c((1, 3), 2)
    step_z(3, 2)
    ready_c(8)
    compute((8,), (0, 1, 2))
    got_c((1, 3), 3)
    got_c((1, 2), 0, 1)
    step_z(3, 3)
    got_c((2, 2), 2, 3)
    ready_r(3, -3)
    compute((0, 1, 2, 3), (3, -3))
    got_c((2, 2), 0, 1)
    ready_c(4, 5)
    compute((4, 5), (0, 1, -1, 2, -2, 3, -3))
    compute((6, 7, 8), (3,))
    got_z(4, 2)
    got_z(4, 0)
    ready_r(4)
    ready_c(9)
    compute((9,), (0, 1, 2, 3))
    every = tuple(range(10))
    half[...] = scores_of(every, (4,), EARLY)
    got_z(4, 3)
    got_z(4, 1)
    half[...] += scores_of(every, (4,), LATE)
    side = acc_r[7]
    for j in range(20):
        side = jnp.maximum(side, split(half[:, j * 128:(j + 1) * 128], 7, j)[0])
    acc_r[7] = side
    answer_r(4)
    for i in (9, 3, 5, 4, 7, 8, 2, 0, 1, 6):
        for j in (2 * i, 2 * i + 1):
            earlier = split(half[:, j * 128:(j + 1) * 128], 7, j)[1]
            acc_c[j] = jnp.maximum(acc_c[j], jnp.max(earlier.reshape(16, 8, 128), axis=0))
        answer_c(i)
        if i == 9:
            answer_r(3, -3)
    answer_r(2, -2, 1, -1, 0)

    for d in sends:
        d.wait_send()
    best = jnp.maximum(out_r[0], acc_c[2 * OWN])
    for u in range(1, 8):
        arrived(res_r.at[u], rsem_r.at[u])
        best = jnp.maximum(best, res_r[u])
    for j in range(20):
        if j != 2 * OWN:
            arrived(res_c.at[j], rsem_c.at[j])
            best = jnp.maximum(best, res_c[j])
    out_ref[...] = jnp.max(best, axis=0, keepdims=True)


def shards(embeddings, cluster_ids, row_order):
    out = pl.pallas_call(
        kernel,
        out_shape=jax.ShapeDtypeStruct((1, 128), jnp.float32),
        in_specs=[pl.BlockSpec(memory_space=pltpu.HBM)] + [pl.BlockSpec(memory_space=pltpu.VMEM)] * 2,
        out_specs=pl.BlockSpec(memory_space=pltpu.VMEM),
        scratch_shapes=[
            pltpu.VMEM((128, 1024), jnp.bfloat16),
            pltpu.SemaphoreType.DMA,
            pltpu.VMEM((20, CHUNKS, 16, 128), jnp.bfloat16),
            pltpu.VMEM((8, CHUNKS, 16, 128), jnp.bfloat16),
            pltpu.VMEM((8, 128, 128), jnp.float32),
            pltpu.VMEM((8, 128, 128), jnp.float32),
            pltpu.VMEM((20, 8, 128), jnp.float32),
            pltpu.VMEM((20, 8, 128), jnp.float32),
            pltpu.VMEM((128, 2560), jnp.float32),
            pltpu.VMEM((8, 128, 128), jnp.float32),
            pltpu.VMEM((20, 8, 128), jnp.float32),
            pltpu.VMEM((8, 8, 128), jnp.float32),
            pltpu.VMEM((8, 8, 128), jnp.float32),
            pltpu.VMEM((20, 8, 128), jnp.float32),
            pltpu.SemaphoreType.DMA((128,)),
            pltpu.SemaphoreType.DMA((10, 4)),
            pltpu.SemaphoreType.DMA((10, 2)),
            pltpu.SemaphoreType.DMA((8, 4)),
            pltpu.SemaphoreType.DMA((8,)),
            pltpu.SemaphoreType.DMA((20,)),
            pltpu.SemaphoreType.REGULAR,
        ],
        compiler_params=pltpu.CompilerParams(collective_id=0, has_side_effects=True, vmem_limit_bytes=56475648),
        name="nearest_earlier",
    )(embeddings, cluster_ids.reshape(1, 128), row_order.reshape(1, 128))
    return out.reshape(128)


def solution(mesh):
    in_specs = (P(("grp", "blk"), None), P(("grp", "blk")), P(("grp", "blk")))
    return jax.shard_map(shards, mesh=mesh, in_specs=in_specs, out_specs=P(("grp", "blk")), check_vma=False)
```

```python
import jax
import jax.numpy as jnp
from jax import lax
from jax.experimental import pallas as pl
from jax.experimental.pallas import tpu as pltpu
from jax.sharding import PartitionSpec as P

MESH = pl.DeviceIdType.MESH
NX, NY, NZ = 4, 4, 8
CHUNKS = 65
HALVES = ((0, 33), (33, 32))
QUARTERS = ((0, 17), (17, 16), (33, 16), (49, 16))
EARLY, LATE = (0, 1, 4, 5), (2, 3, 6, 7)
PLANE = ((1, 0), (0, 1), (3, 3), (2, 3), (1, 3), (1, 2), (0, 0), (0, 2), (2, 0), (2, 2))
OWN = PLANE.index((0, 0))
COLUMN = (0, 1, -1, 2, -2, 3, -3, 4)
ONWARD = {
    (0, 0): (((-1, 0), (0, 1, 2, 3)), ((0, -1), (2, 3, 0, 1))),
    (1, 0): (((-1, 0), (0, 1)), ((0, 1), (0, 1))),
    (0, 1): (((0, -1), (0, 1, 2, 3)),),
    (0, 2): (((-1, 0), (0, 1, 2, 3)),),
    (3, 3): (((1, 0), (0, 1, 2, 3)),),
    (2, 3): (((1, 0), (2, 3)), ((0, -1), (2, 3)), ((0, 1), (0, 1, 2, 3))),
}


def rows_of(R, u, features=range(8)):
    return jnp.concatenate([R[u, 1 + k * 8:9 + k * 8].reshape(128, 128) for k in features], axis=1)


def columns_of(C, j, features=range(8)):
    return jnp.concatenate([C[j, 1 + k * 8:9 + k * 8].reshape(128, 128) for k in features], axis=0)


def product(rows, columns):
    return jnp.dot(rows, columns, preferred_element_type=jnp.float32)


def keys_of(tag):
    tag = tag.astype(jnp.float32)
    low = tag[0:1] * 32768.0
    return low, low + tag[1:2] * 256.0 + tag[2:3]


def kernel(emb_hbm, cid_ref, ord_ref, out_ref, emb_ref, in_sem, C, R, row_low, row_key, low_key, high_key, half, acc_r, acc_c, out_r, res_r, res_c, send_sems, csem, ssem, zsem, rsem_r, rsem_c, corner_sem):
    load = pltpu.make_async_copy(emb_hbm, emb_ref, in_sem)
    load.start()
    x = lax.axis_index("grp")
    blk = lax.axis_index("blk")
    core = lax.rem(blk, 2)
    y = lax.rem(lax.div(blk, 2), NY)
    z = lax.div(blk, 2 * NY)

    def dev(dx, dy, dz, dc):
        other = lax.rem(core + dc, 2)
        return (lax.rem(x + dx % NX, NX), (lax.rem(z + dz % NZ, NZ) * NY + lax.rem(y + dy % NY, NY)) * 2 + other)

    sib = dev(0, 0, 0, 1)

    barrier = pltpu.get_barrier_semaphore()
    near = [dev(1, 0, 0, 0), dev(-1, 0, 0, 0), dev(0, 1, 0, 0), dev(0, -1, 0, 0), dev(0, 0, 1, 0), dev(0, 0, -1, 0), sib]
    for target in near:
        pl.semaphore_signal(barrier, inc=1, device_id=target, device_id_type=MESH)

    load.wait()
    values = emb_ref[...].astype(jnp.float32)
    total = jnp.sum(values * values, axis=1, keepdims=True)
    unit = values * lax.rsqrt(total + 1e-06)
    for k in range(8):
        R[0, 1 + k * 8:9 + k * 8] = unit[:, k * 128:(k + 1) * 128].astype(jnp.bfloat16).reshape(8, 16, 128)
    row = lax.broadcasted_iota(jnp.int32, (16, 128), 0)
    order = ord_ref[...]
    tag = jnp.where(row == 0, cid_ref[...], jnp.where(row == 1, lax.shift_right_logical(order, 8), jnp.where(row == 2, order & 255, 0)))
    tag = tag.astype(jnp.float32).astype(jnp.bfloat16)
    C[2 * OWN, 0] = tag
    R[0, 0] = tag
    pl.semaphore_wait(barrier, len(near))

    sends = []

    def copy(src, dst, sem, target):
        d = pltpu.make_async_remote_copy(
            src_ref=src, dst_ref=dst, send_sem=send_sems.at[len(sends)], recv_sem=sem, device_id=target, device_id_type=MESH
        )
        d.start()
        sends.append(d)

    def arrived(dst, sem):
        pltpu.make_async_remote_copy(
            src_ref=dst, dst_ref=dst, send_sem=send_sems.at[0], recv_sem=sem, device_id=sib, device_id_type=MESH
        ).wait_recv()

    def cpart(i, q):
        return C.at[2 * i, pl.ds(*QUARTERS[q])]

    def zpart(u, q):
        return R.at[u, pl.ds(*QUARTERS[q])]

    def pass_c(d, step, q):
        i = PLANE.index(d)
        j = PLANE.index(((d[0] - step[0]) % NX, (d[1] - step[1]) % NY))
        copy(cpart(i, q), cpart(j, q), csem.at[j, q], dev(step[0], step[1], 0, 0))

    def share(i, h):
        copy(C.at[2 * i, pl.ds(*HALVES[h])], C.at[2 * i + 1, pl.ds(*HALVES[h])], ssem.at[i, h], sib)

    def got_c(d, *quarters):
        i = PLANE.index(d)
        for q in quarters:
            arrived(cpart(i, q), csem.at[i, q])
            for step, some in ONWARD.get(d, ()):
                if q in some:
                    pass_c(d, step, q)
            if q % 2:
                share(i, q // 2)

    def pass_z(k, q, steps=(1, -1)):
        i = COLUMN.index(k)
        for step in steps:
            if k * step > 0 or (abs(k) == 3 and q // 2 != (step + 1) // 2):
                continue
            to = k - step
            j = COLUMN.index(4 if abs(to) == 4 else to)
            copy(zpart(i, q), zpart(j, q), zsem.at[j, q], dev(0, 0, step, 0))

    def got_z(k, q):
        j = COLUMN.index(k)
        arrived(zpart(j, q), zsem.at[j, q])
        if k != 4:
            pass_z(k, q)

    def step_z(k, n):
        got_z(-k, (n + 2) % 4)
        got_z(k, n)

    def ready_c(*blocks):
        for i in blocks:
            for h in range(2):
                arrived(C.at[2 * i + 1, pl.ds(*HALVES[h])], ssem.at[i, h])
            for j in (2 * i, 2 * i + 1):
                low, high = keys_of(C[j, 0])
                low_key[j, 0:1, :] = low
                high_key[j, 0:1, :] = high

    def ready_r(*ks):
        for k in ks:
            u = COLUMN.index(k)
            low, high = keys_of(R[u, 0])
            row_low[u] = jnp.broadcast_to(low, (128, 128)).T
            row_key[u] = jnp.broadcast_to(high, (128, 128)).T

    def split(part, u, j):
        same = jnp.where(row_low[u] == low_key[j, 0:1, :], part, jnp.float32(-1.0))
        high = high_key[j, 0:1, :]
        before = row_key[u] < high
        if (u, j) == (0, 2 * OWN):
            return jnp.where(row_key[u] > high, same, jnp.float32(-1.0)), jnp.where(before, same, jnp.float32(-1.0))
        return jnp.where(before, jnp.float32(-1.0), same), jnp.where(before, same, jnp.float32(-1.0))

    def use(scores, blocks, ks):
        for a, k in enumerate(ks):
            u = COLUMN.index(k)
            side = acc_r[u]
            for b in range(2 * len(blocks)):
                j = 2 * blocks[b // 2] + b % 2
                later, earlier = split(scores[a * 128:(a + 1) * 128, b * 128:(b + 1) * 128], u, j)
                acc_c[j] = jnp.maximum(acc_c[j], jnp.max(earlier.reshape(16, 8, 128), axis=0))
                side = jnp.maximum(side, later)
            acc_r[u] = side

    def scores_of(blocks, ks, features=range(8)):
        rows = jnp.concatenate([rows_of(R, COLUMN.index(k), features) for k in ks], axis=0)
        columns = jnp.concatenate([columns_of(C, 2 * i + c, features) for i in blocks for c in range(2)], axis=1)
        return product(rows, columns)

    def compute(blocks, ks):
        use(scores_of(blocks, ks), blocks, ks)

    def answer_r(*ks):
        for k in ks:
            u = COLUMN.index(k)
            out_r[u] = jnp.max(acc_r[u].T.reshape(16, 8, 128), axis=0)
            if k:
                v = COLUMN.index(4 if k == 4 else -k)
                copy(out_r.at[u], res_r.at[v], rsem_r.at[v], dev(0, 0, k, 0))

    def answer_c(*blocks):
        for i in blocks:
            for c in range(2):
                j = 2 * i + c
                if j != 2 * OWN:
                    copy(acc_c.at[j], res_c.at[j], rsem_c.at[j], dev(PLANE[i][0], PLANE[i][1], 0, c))

    pl.semaphore_signal(corner_sem, inc=1, device_id=dev(-1, 0, 0, 0), device_id_type=MESH)

    for q in range(4):
        pass_z(0, (q + 2) % 4, (1,))
        pass_z(0, q, (-1,))
    for k in range(8):
        C[2 * OWN, 1 + k * 8:9 + k * 8] = unit[:, k * 128:(k + 1) * 128].T.astype(jnp.bfloat16).reshape(8, 16, 128)
    for q in range(4):
        for step, order in ONWARD[(0, 0)]:
            pass_c((0, 0), step, order[q])
    share(OWN, 0)
    share(OWN, 1)
    acc_r[...] = jnp.full(acc_r.shape, -1.0, jnp.float32)
    acc_c[...] = jnp.full(acc_c.shape, -1.0, jnp.float32)
    pl.semaphore_wait(corner_sem, 1)
    for q in (2, 3, 0, 1):
        pass_c((0, 0), (1, 1), q)

    step_z(1, 0)
    got_c((1, 0), 0)
    got_c((0, 1), 2)
    step_z(1, 1)
    got_c((1, 0), 1)
    got_c((0, 1), 3)
    got_c((3, 3), 2)
    step_z(1, 2)
    got_c((0, 1), 0)
    got_c((1, 0), 2)
    got_c((3, 3), 3)
    step_z(1, 3)
    got_c((0, 1), 1)
    got_c((1, 0), 3)
    got_c((3, 3), 0)
    ready_r(0, 1, -1)
    ready_c(OWN)
    step_z(2, 0)
    got_c((0, 2), 2)
    got_c((3, 3), 1)
    ready_c(0, 1)
    compute((6, 0, 1), (0, 1, -1))
    step_z(2, 1)
    got_c((2, 3), 2)
    got_c((0, 2), 3)
    ready_c(2)
    step_z(2, 2)
    compute((2,), (0, 1, -1))
    got_c((2, 3), 3)
    got_c((0, 2), 0)
    got_c((2, 3), 0)
    step_z(2, 3)
    got_c((0, 2), 1)
    ready_r(2, -2)
    compute((6, 0, 1, 2), (2, -2))
    got_c((2, 3), 1)
    got_c((1, 3), 0, 1)
    step_z(3, 0)
    ready_c(7)
    compute((7,), (0, 1, 2))
    got_c((2, 0), 0, 1, 2)
    got_c((1, 2), 2)
    step_z(3, 1)
    ready_c(3)
    compute((3,), (0, 1, -1, 2, -2))
    got_c((2, 0), 3)
    got_c((1, 2), 3)
    got_c((1, 3), 2)
    step_z(3, 2)
    ready_c(8)
    compute((8,), (0, 1, 2))
    got_c((1, 3), 3)
    got_c((1, 2), 0, 1)
    step_z(3, 3)
    got_c((2, 2), 2, 3)
    ready_r(3, -3)
    compute((0, 1, 2, 3), (3, -3))
    got_c((2, 2), 0, 1)
    ready_c(4, 5)
    compute((4, 5), (0, 1, -1, 2, -2, 3, -3))
    compute((6, 7, 8), (3,))
    got_z(4, 2)
    got_z(4, 0)
    ready_r(4)
    ready_c(9)
    compute((9,), (0, 1, 2, 3))
    every = tuple(range(10))
    half[...] = scores_of(every, (4,), EARLY)
    got_z(4, 3)
    got_z(4, 1)
    half[...] += scores_of(every, (4,), LATE)
    side = acc_r[7]
    for j in range(20):
        side = jnp.maximum(side, split(half[:, j * 128:(j + 1) * 128], 7, j)[0])
    acc_r[7] = side
    answer_r(4)
    for i in (9, 3, 5, 4, 7, 8, 2, 0, 1, 6):
        for j in (2 * i, 2 * i + 1):
            earlier = split(half[:, j * 128:(j + 1) * 128], 7, j)[1]
            acc_c[j] = jnp.maximum(acc_c[j], jnp.max(earlier.reshape(16, 8, 128), axis=0))
        answer_c(i)
        if i == 5:
            answer_r(3, -3)
    answer_r(2, -2, 1, -1, 0)

    for d in sends:
        d.wait_send()
    best = jnp.maximum(out_r[0], acc_c[2 * OWN])
    for u in range(1, 8):
        arrived(res_r.at[u], rsem_r.at[u])
        best = jnp.maximum(best, res_r[u])
    for j in range(20):
        if j != 2 * OWN:
            arrived(res_c.at[j], rsem_c.at[j])
            best = jnp.maximum(best, res_c[j])
    out_ref[...] = jnp.max(best, axis=0, keepdims=True)


def shards(embeddings, cluster_ids, row_order):
    out = pl.pallas_call(
        kernel,
        out_shape=jax.ShapeDtypeStruct((1, 128), jnp.float32),
        in_specs=[pl.BlockSpec(memory_space=pltpu.HBM)] + [pl.BlockSpec(memory_space=pltpu.VMEM)] * 2,
        out_specs=pl.BlockSpec(memory_space=pltpu.VMEM),
        scratch_shapes=[
            pltpu.VMEM((128, 1024), jnp.bfloat16),
            pltpu.SemaphoreType.DMA,
            pltpu.VMEM((20, CHUNKS, 16, 128), jnp.bfloat16),
            pltpu.VMEM((8, CHUNKS, 16, 128), jnp.bfloat16),
            pltpu.VMEM((8, 128, 128), jnp.float32),
            pltpu.VMEM((8, 128, 128), jnp.float32),
            pltpu.VMEM((20, 8, 128), jnp.float32),
            pltpu.VMEM((20, 8, 128), jnp.float32),
            pltpu.VMEM((128, 2560), jnp.float32),
            pltpu.VMEM((8, 128, 128), jnp.float32),
            pltpu.VMEM((20, 8, 128), jnp.float32),
            pltpu.VMEM((8, 8, 128), jnp.float32),
            pltpu.VMEM((8, 8, 128), jnp.float32),
            pltpu.VMEM((20, 8, 128), jnp.float32),
            pltpu.SemaphoreType.DMA((128,)),
            pltpu.SemaphoreType.DMA((10, 4)),
            pltpu.SemaphoreType.DMA((10, 2)),
            pltpu.SemaphoreType.DMA((8, 4)),
            pltpu.SemaphoreType.DMA((8,)),
            pltpu.SemaphoreType.DMA((20,)),
            pltpu.SemaphoreType.REGULAR,
        ],
        compiler_params=pltpu.CompilerParams(collective_id=0, has_side_effects=True, vmem_limit_bytes=56475648),
        name="nearest_earlier",
    )(embeddings, cluster_ids.reshape(1, 128), row_order.reshape(1, 128))
    return out.reshape(128)


def solution(mesh):
    in_specs = (P(("grp", "blk"), None), P(("grp", "blk")), P(("grp", "blk")))
    return jax.shard_map(shards, mesh=mesh, in_specs=in_specs, out_specs=P(("grp", "blk")), check_vma=False)
```
